256 devices in a mesh: tm: 32 (over z, x), space: 8 (over y, core).
Axes of the slice: x: 4, y: 4, z: 8, core: 2. Of those that a mesh axis runs over, the one named last changes fastest.
Arguments:
- initial: float32 [64, 2048], P('space'), may hold values from -6 to 6
- source: float32 [64, 2048], P('space'), may hold values from -3 to 3
- diff_rate: float32 [64, 2048], P('space'), may hold values from 0.004 to 0.04
- vel_x: float32 [64, 2048], P('space'), may hold values from -0.04 to 0.04
- vel_y: float32 [64, 2048], P('space'), may hold values from -0.04 to 0.04
- amp: float32 [256], P('tm'), may hold values from 0.5 to 1.5
- c_guess: float32 [64, 64, 2048], P('tm', 'space'), may hold values from -6 to 6
Outputs:
- corrected: float32 [64, 64, 2048], P('tm', 'space')
The draws below stay inside these ranges and needn't reach their ends.
All inputs are finite; a program needn't handle non-finite values.
Results may differ from the reference program's by a relative error of at most 0.00002.
Values sent between devices are 32-bit elements; how exact they have to be, the bound alone decides.
A program may use at most 64 MiB of HBM per device.

```python
import math
import jax
import jax.numpy as jnp
from jax import lax

NY = 2048
M = 4
NX = 64
NC = 64
NT = 256


def steps_of(rng, shape, shards, smallest, top_value):
    level, own = 1.0, jax.random.fold_in(rng, 6)
    for position, parts in shards:
        steps = jnp.exp(jax.random.uniform(jax.random.fold_in(own, position), (parts,), jnp.float32, smallest / len(shards), top_value / len(shards)))
        level = level * jnp.repeat(steps, shape[position] // parts).reshape([-1 if axis == position else 1 for axis in range(len(shape))])
    return level


def scatter_about(key, shape, scale, most, split=(), held_as=jnp.bfloat16):
    entries = jax.random.normal(key, shape, jnp.float32) * scale
    if len(split) > 0:
        entries = steps_of(key, shape, split, -0.22, 0.18) * entries
    return jnp.clip(entries, min=-most, max=most).astype(held_as)


def setup_inputs(seed: int = 0) -> dict:
    key_list = jax.random.split(jax.random.key(seed), 8)
    return {
        "initial": scatter_about(key_list[0], (NX, NY), 1.0, 6.0, ((0, 8),), jnp.float32),
        "source": scatter_about(key_list[1], (NX, NY), 0.2, 3.0, ((0, 8),), jnp.float32),
        "diff_rate": jnp.clip(jnp.exp(math.log(0.04) - 2.30258502 * jax.random.uniform(key_list[2], (NX, NY), jnp.float32) ** steps_of(key_list[2], (NX, NY), ((0, 8),), -0.2, 0.2)), 0.004, 0.04),
        "vel_x": jnp.clip(jax.random.uniform(key_list[3], (NX, NY), jnp.float32, -0.04, 0.04) * steps_of(key_list[3], (NX, NY), ((0, 8),), -0.4, 0.0), -0.04, 0.04),
        "vel_y": jnp.clip(jax.random.uniform(key_list[4], (NX, NY), jnp.float32, -0.04, 0.04) * steps_of(key_list[4], (NX, NY), ((0, 8),), -0.4, 0.0), -0.04, 0.04),
        "amp": jnp.clip(0.5 + 1.0 * jax.random.uniform(key_list[5], (NT,), jnp.float32) ** steps_of(key_list[5], (NT,), ((0, 32),), -0.2, 0.2), 0.5, 1.5),
        "c_guess": scatter_about(key_list[6], (NC, NX, NY), 1.0, 6.0, ((0, 32), (1, 8)), jnp.float32),
    }


def advance(field, rate, along_x, along_y):
    padded = jnp.pad(field, ((0, 0), (1, 1), (1, 1)))
    row_up = padded[:, 2:, 1:-1]
    row_down = padded[:, :-2, 1:-1]
    col_up = padded[:, 1:-1, 2:]
    col_down = padded[:, 1:-1, :-2]
    spread = rate * (row_up + row_down + col_up + col_down - 4.0 * field)
    drift_x = jnp.maximum(along_x, 0.0) * (field - row_down) + jnp.minimum(along_x, 0.0) * (row_up - field)
    drift_y = jnp.maximum(along_y, 0.0) * (field - col_down) + jnp.minimum(along_y, 0.0) * (col_up - field)
    return field + spread - drift_x - drift_y


def propagate(starts, amps, source, diff_rate, vel_x, vel_y):
    state = starts
    for step_index in range(M):
        state = advance(state, diff_rate, vel_x, vel_y) + amps[:, step_index][:, None, None] * source[None]
    return state


def reference(initial, source, diff_rate, vel_x, vel_y, amp, c_guess):
    amps = amp.reshape(NC, M)
    starts_first = jnp.concatenate([initial[None], c_guess[:-1]], axis=0)
    relaxed = propagate(starts_first, amps, source, diff_rate, vel_x, vel_y)
    starts_second = jnp.concatenate([initial[None], relaxed[:-1]], axis=0)
    resid = propagate(starts_second, amps, source, diff_rate, vel_x, vel_y) - relaxed
    coarse_rate = M * diff_rate
    coarse_x = M * vel_x
    coarse_y = M * vel_y

    def coarse_body(error, term):
        error = advance(error[None], coarse_rate, coarse_x, coarse_y)[0] + term
        return error, error

    _, errors = lax.scan(coarse_body, jnp.zeros((NX, NY), jnp.float32), resid)
    return relaxed + errors
```

```python
import functools

import jax
import jax.numpy as jnp
from jax import lax
from jax.experimental import pallas as pl
from jax.experimental.pallas import tpu as pltpu
from jax.sharding import PartitionSpec as P

M = 4
NZ = 8
NX_DEV = 4
NS = 8
STRIPS = 32
LANES = 128


def place_of(strip):
    chip, core = strip // 2, strip % 2
    y, q = chip // 4, chip % 4
    x = q + (y % 2) * (3 - 2 * q)
    return x, 2 * y + core


def strip_of(x, s):
    y, core = s // 2, s % 2
    q = x + (y % 2) * (3 - 2 * x)
    return 2 * (4 * y + q) + core


def lane_ids(rows):
    return lax.broadcasted_iota(jnp.int32, (rows, LANES), 1)


def pack_halves(value, out_ref):
    lane = lane_ids(16)
    for half in range(2):
        block = 1 + half
        packed = None
        for group in range(4):
            piece = value[16 * group : 16 * group + 16]
            shift = (32 * (group - block)) % LANES
            moved = piece if shift == 0 else pltpu.roll(piece, shift, 1)
            packed = moved if packed is None else jnp.where(lane < 32 * group, packed, moved)
        out_ref[half] = packed


def unpack_window(parts):
    lane = lane_ids(16)
    rows = []
    for group in range(4):
        row = None
        for block in range(4):
            shift = (32 * (block - group)) % LANES
            moved = parts[block] if shift == 0 else pltpu.roll(parts[block], shift, 1)
            row = moved if row is None else jnp.where(lane < 32 * block, row, moved)
        rows.append(row)
    return jnp.concatenate(rows, axis=0)


def stencil(cf, base, u):
    near = cf[base] * u + cf[base + 1] * pltpu.roll(u, 1, 0) + cf[base + 2] * pltpu.roll(u, 63, 0)
    return near + (cf[base + 3] * pltpu.roll(u, 1, 1) + cf[base + 4] * pltpu.roll(u, 127, 1))


def kernel(
    initial, source, rate, velx, vely, strengths, guess, out,
    amp, gb, fb, ib, sb, sp, rb, pb, cf, rx, rd, eb, pk, pe, lr, po, ob,
    ld, s1, r1, sq, rq, s2, r2, s3, r3,
):
    t, s = lax.axis_index("tm"), lax.axis_index("space")
    z, x = t // NX_DEV, t % NX_DEV
    c = strip_of(x, s)
    c_lo, c_hi = (c + STRIPS - 1) % STRIPS, (c + 1) % STRIPS
    zn = (z + 1) % NZ
    last_x = x == NX_DEV - 1

    def at(plane, strip):
        px, ps = place_of(strip)
        return (plane * NX_DEV + px, ps)

    barrier = pltpu.get_barrier_semaphore()

    def greet(device):
        pl.semaphore_signal(barrier, inc=1, device_id=device, device_id_type=pl.DeviceIdType.MESH)

    def greet_mate(i, _):
        greet(at(z, (c + i) % STRIPS))
        return 0

    lax.fori_loop(1, STRIPS, greet_mate, 0)

    def greet_before(i, _):
        greet((((z + NZ - 1) % NZ) * NX_DEV + NX_DEV - 1, i))
        return 0

    lax.fori_loop(0, NS, greet_before, 0)

    def greet_earlier(j, _):
        greet(at(z - j, c_lo))
        greet(at(z - j, c))
        greet(at(z - j, c_hi))
        return 0

    lax.fori_loop(1, 1 + jnp.minimum(z, 4), greet_earlier, 0)

    load_guess = pltpu.make_async_copy(guess, gb, ld.at[0])
    load_guess.start()
    load_amp = pltpu.make_async_copy(strengths, amp, ld.at[3])
    load_amp.start()
    for which, field in enumerate((rate, velx, vely, source)):

        @pl.when(x == which)
        def _(field=field):
            pltpu.make_async_copy(field, fb, ld.at[1]).start()

    @pl.when(jnp.logical_and(last_x, z == NZ - 1))
    def _():
        pltpu.make_async_copy(initial, ib, ld.at[2]).start()

    @pl.when(jnp.logical_and(last_x, z < NZ - 1))
    def _():
        pltpu.make_async_copy(guess.at[1], ib, ld.at[2]).start()

    load_guess.wait()
    load_amp.wait()
    pltpu.make_async_copy(rate, fb, ld.at[1]).wait()

    lane8 = lane_ids(8)

    def windows(tile_of, put):
        low = [pltpu.roll(tile_of(k), 32, 1) for k in range(16)]
        for k in range(16):
            put(2 * k, jnp.where(lane8 < 32, low[k - 1], low[k]))
        high = [pltpu.roll(tile_of(k), 96, 1) for k in range(16)]
        for k in range(16):
            put(2 * k + 1, jnp.where(lane8 < 96, high[k], high[(k + 1) % 16]))

    for i in range(2):

        def put_guess(strip, value, i=i):
            for m in range(M):
                value = jnp.where(lane8 == m, amp[M * i + m], value)
            sb[strip, i] = value

        windows(lambda k, i=i: gb[i, :, LANES * k : LANES * (k + 1)], put_guess)

    def put_field(strip, value):
        sb[strip, 2] = value

    windows(lambda k: fb[:, LANES * k : LANES * (k + 1)], put_field)

    @pl.when(last_x)
    def _():
        pltpu.make_async_copy(initial, ib, ld.at[2]).wait()

        def put_before(strip, value):
            sp[strip] = value

        windows(lambda k: ib[:, LANES * k : LANES * (k + 1)], put_before)

    pl.semaphore_wait(
        barrier, STRIPS - 1 + jnp.where(last_x, STRIPS, 0) + 3 * jnp.minimum(NZ - 1 - z, 4)
    )

    mine = rb.at[pl.ds(3 * x, 3), pl.ds(8 * s, 8)]

    @pl.when(last_x)
    def _():
        def send_before(i, _):
            strip = (c + i) % STRIPS
            pltpu.make_async_remote_copy(
                sp.at[strip], pb.at[pl.ds(8 * s, 8)], sq, rq, at(zn, strip), pl.DeviceIdType.MESH
            ).start()
            return 0

        lax.fori_loop(0, STRIPS, send_before, 0)

    def send_mate(i, _):
        strip = (c + i) % STRIPS
        pltpu.make_async_remote_copy(
            sb.at[strip], mine, s1, r1, at(z, strip), pl.DeviceIdType.MESH
        ).start()
        return 0

    lax.fori_loop(1, STRIPS, send_mate, 0)
    pltpu.make_async_copy(sb.at[c], mine, r1).start()
    pltpu.make_async_copy(rb, rb, r1).wait()

    d, a, b = rb[2], rb[5], rb[8]
    row = lax.broadcasted_iota(jnp.int32, (64, LANES), 0)
    col = lax.broadcasted_iota(jnp.int32, (64, LANES), 1) + (64 * c - 32)
    zero = jnp.zeros((64, LANES), jnp.float32)
    c_mid = 1.0 - (4.0 * d + (jnp.abs(a) + jnp.abs(b)))
    c_xm = jnp.where(row == 0, zero, d + jnp.maximum(a, 0.0))
    c_xp = jnp.where(row == 63, zero, d - jnp.minimum(a, 0.0))
    c_ym = jnp.where(col == 0, zero, d + jnp.maximum(b, 0.0))
    c_yp = jnp.where(col == 2047, zero, d - jnp.minimum(b, 0.0))
    cf[0], cf[1], cf[2], cf[3], cf[4] = c_mid, c_xm, c_xp, c_ym, c_yp
    cf[5] = 1.0 - float(M) * (4.0 * d + (jnp.abs(a) + jnp.abs(b)))
    cf[6], cf[7], cf[8], cf[9] = M * c_xm, M * c_xp, M * c_ym, M * c_yp

    pltpu.make_async_copy(pb, pb, rq).wait()

    def forced(u, tile, m):
        strength = jnp.broadcast_to(rb[tile, 0:8, m : m + 1], (8, LANES))
        push = rb[11].reshape(8, 8, LANES) * strength[None]
        return stencil(cf, 0, u) + push.reshape(64, LANES)

    def fine_pair(xx, first):
        tile = 3 * xx
        u, v = first, rb[tile]
        for m in range(M):
            u = forced(u, tile, m)
            v = forced(v, tile + 1, m)
        rx[2 * xx], rx[2 * xx + 1] = u, v
        u, v = u - rb[tile], v - rb[tile + 1]
        for m in range(M):
            u = stencil(cf, 0, u)
            v = stencil(cf, 0, v)
        rd[2 * xx], rd[2 * xx + 1] = u, v
        return rb[tile + 1]

    lax.fori_loop(0, NX_DEV, fine_pair, pb[...])

    def coarse_local(k, err):
        return stencil(cf, 5, err) + rd[k]

    def coarse_power(err):
        return lax.fori_loop(0, 8, lambda k, v: stencil(cf, 5, v), err)

    entry = jnp.where(z == 0, rx[0] - rx[0], zero)
    eb[...] = entry
    local_last = lax.fori_loop(0, 8, coarse_local, entry)
    pack_halves(local_last, pk)

    def send_three(packed, plane, slot):
        for src, dst, strip in ((packed, lr.at[slot, pl.ds(1, 2)], c), (packed.at[0], lr.at[slot, 3], c_lo), (packed.at[1], lr.at[slot, 0], c_hi)):
            pltpu.make_async_remote_copy(
                src, dst, s2.at[slot], r2.at[slot], at(plane, strip), pl.DeviceIdType.MESH
            ).start()

    @pl.when(z == 0)
    def _():
        send_three(pk, z + 4, 0)

    for j in range(3, 0, -1):

        @pl.when(z + j < NZ)
        def _(j=j):
            send_three(pk, z + j, j)

    @pl.when(z >= 4)
    def _():
        pltpu.make_async_copy(lr.at[0], lr.at[0], r2.at[0]).wait()
        eb[...] = unpack_window([lr[0, h] for h in range(4)])

    for j in range(3, 0, -1):

        @pl.when(z - j >= 0)
        def _(j=j):
            pltpu.make_async_copy(lr.at[j], lr.at[j], r2.at[j]).wait()
            part = unpack_window([lr[j, h] for h in range(4)])
            steps = jnp.where(z - j > 0, 8, 0)
            eb[...] = part + lax.fori_loop(0, steps, lambda k, v: stencil(cf, 5, v), eb[...])

    lane64 = lane_ids(64)
    err = eb[...]
    for xx in range(NX_DEV):
        first = rx[2 * xx] + err
        err = coarse_local(2 * xx, err)
        second = rx[2 * xx + 1] + err
        err = coarse_local(2 * xx + 1, err)
        po[xx] = jnp.where(lane64 < 64, pltpu.roll(first, 96, 1), pltpu.roll(second, 32, 1))

    @pl.when(jnp.logical_and(z >= 1, z <= 3))
    def _():
        pack_halves(err, pe)
        send_three(pe, z + 4, 0)

    def send_out(i, _):
        xx, ss = place_of((c + i) % STRIPS)
        pltpu.make_async_remote_copy(
            po.at[xx, pl.ds(8 * ss, 8)], ob.at[c], s3, r3, (z * NX_DEV + xx, ss), pl.DeviceIdType.MESH
        ).start()
        return 0

    lax.fori_loop(1, STRIPS, send_out, 0)
    pltpu.make_async_copy(po.at[x, pl.ds(8 * s, 8)], ob.at[c], r3).start()
    pltpu.make_async_copy(ob, ob, r3).wait()

    for p in range(16):
        left, right = ob[2 * p], ob[2 * p + 1]
        here = slice(LANES * p, LANES * (p + 1))
        out[0, :, here] = jnp.where(lane8 < 64, left, pltpu.roll(right, 64, 1))
        out[1, :, here] = jnp.where(lane8 < 64, pltpu.roll(left, 64, 1), right)

    sent = sb.at[pl.ds(0, STRIPS - 1)]
    pltpu.make_async_copy(sent, sent, s1).wait()

    @pl.when(last_x)
    def _():
        pltpu.make_async_copy(sp, sp, sq).wait()

    @pl.when(z <= 3)
    def _():
        pltpu.make_async_copy(lr.at[0], lr.at[0], s2.at[0]).wait()

    for j in range(1, 4):

        @pl.when(z + j < NZ)
        def _(j=j):
            pltpu.make_async_copy(lr.at[j], lr.at[j], s2.at[j]).wait()

    gone = ob.at[pl.ds(0, STRIPS - 1)]
    pltpu.make_async_copy(gone, gone, s3).wait()


def per_device(*blocks):
    any_space = pl.BlockSpec(memory_space=pl.ANY)
    f32 = functools.partial(pltpu.VMEM, dtype=jnp.float32)
    sem = pltpu.SemaphoreType.DMA
    return pl.pallas_call(
        kernel,
        out_shape=jax.ShapeDtypeStruct((2, 8, 2048), jnp.float32),
        in_specs=[any_space] * 7,
        out_specs=pl.BlockSpec(memory_space=pltpu.VMEM),
        scratch_shapes=[
            pltpu.SMEM((8,), jnp.float32),
            f32((2, 8, 2048)),
            f32((8, 2048)),
            f32((8, 2048)),
            f32((STRIPS, 3, 8, LANES)),
            f32((STRIPS, 8, LANES)),
            f32((12, 64, LANES)),
            f32((64, LANES)),
            f32((10, 64, LANES)),
            f32((8, 64, LANES)),
            f32((8, 64, LANES)),
            f32((64, LANES)),
            f32((2, 16, LANES)),
            f32((2, 16, LANES)),
            f32((4, 4, 16, LANES)),
            f32((NX_DEV, 64, LANES)),
            f32((STRIPS, 8, LANES)),
            sem((4,)),
            sem,
            sem,
            sem,
            sem,
            sem((4,)),
            sem((4,)),
            sem,
            sem,
        ],
        compiler_params=pltpu.CompilerParams(
            collective_id=0, has_side_effects=True, vmem_limit_bytes=56 * 1024 * 1024
        ),
        cost_estimate=pl.CostEstimate(flops=20_000_000, bytes_accessed=700_000, transcendentals=0),
        name="cycle",
    )(*blocks)


def solution(mesh):
    in_specs = (
        P("space", None),
        P("space", None),
        P("space", None),
        P("space", None),
        P("space", None),
        P("tm"),
        P("tm", "space", None),
    )
    out_specs = P("tm", "space", None)
    return jax.shard_map(
        per_device, mesh=mesh, in_specs=in_specs, out_specs=out_specs, check_vma=False
    )
```

```python
import functools

import jax
import jax.numpy as jnp
from jax import lax
from jax.experimental import pallas as pl
from jax.experimental.pallas import tpu as pltpu
from jax.sharding import PartitionSpec as P

M = 4
NZ = 8
NX_DEV = 4
NS = 8
STRIPS = 32
LANES = 128


def place_of(strip):
    chip, core = strip // 2, strip % 2
    y, q = chip // 4, chip % 4
    x = q + (y % 2) * (3 - 2 * q)
    return x, 2 * y + core


def strip_of(x, s):
    y, core = s // 2, s % 2
    q = x + (y % 2) * (3 - 2 * x)
    return 2 * (4 * y + q) + core


def lane_ids(rows):
    return lax.broadcasted_iota(jnp.int32, (rows, LANES), 1)


def pack_halves(value, out_ref):
    lane = lane_ids(16)
    for half in range(2):
        block = 1 + half
        packed = None
        for group in range(4):
            piece = value[16 * group : 16 * group + 16]
            shift = (32 * (group - block)) % LANES
            moved = piece if shift == 0 else pltpu.roll(piece, shift, 1)
            packed = moved if packed is None else jnp.where(lane < 32 * group, packed, moved)
        out_ref[half] = packed


def unpack_window(parts):
    lane = lane_ids(16)
    rows = []
    for group in range(4):
        row = None
        for block in range(4):
            shift = (32 * (block - group)) % LANES
            moved = parts[block] if shift == 0 else pltpu.roll(parts[block], shift, 1)
            row = moved if row is None else jnp.where(lane < 32 * block, row, moved)
        rows.append(row)
    return jnp.concatenate(rows, axis=0)


def point(cf, base, mid, left, right):
    near = cf[base] * mid + cf[base + 1] * pltpu.roll(mid, 1, 0) + cf[base + 2] * pltpu.roll(mid, 63, 0)
    return near + (cf[base + 3] * left + cf[base + 4] * right)


def lanes(u, steps):
    return pltpu.roll(u, steps % LANES, 1)


def stencil(cf, base, u):
    return point(cf, base, u, lanes(u, 1), lanes(u, -1))


def coarse_two(cf, u, r1=None, r2=None):
    left, left2, right, right2 = lanes(u, 1), lanes(u, 2), lanes(u, -1), lanes(u, -2)
    v = point(cf, 5, u, left, right)
    v_left = point(cf, 10, left, left2, u)
    v_right = point(cf, 15, right, u, right2)
    if r1 is not None:
        v, v_left, v_right = v + r1, v_left + lanes(r1, 1), v_right + lanes(r1, -1)
    w = point(cf, 5, v, v_left, v_right)
    if r2 is not None:
        w = w + r2
    return v, w


def coarse_eight(cf, u):
    def body(i, u):
        for _ in range(2):
            u = coarse_two(cf, u)[1]
        return u

    return lax.fori_loop(0, 2, body, u)


def kernel(
    initial, source, rate, velx, vely, strengths, guess, ob,
    amp, gb, fb, ib, sb, sp, rb, pb, cf, rx, rd, eb, pk, pe, lr, ul, po,
    ld, s1, r1, sq, rq, s2, r2, s3, r3,
):
    t, s = lax.axis_index("tm"), lax.axis_index("space")
    z, x = t // NX_DEV, t % NX_DEV
    c = strip_of(x, s)
    c_lo, c_hi = (c + STRIPS - 1) % STRIPS, (c + 1) % STRIPS
    zn = (z + 1) % NZ
    last_x = x == NX_DEV - 1

    def at(plane, strip):
        px, ps = place_of(strip)
        return (plane * NX_DEV + px, ps)

    barrier = pltpu.get_barrier_semaphore()

    def greet(device):
        pl.semaphore_signal(barrier, inc=1, device_id=device, device_id_type=pl.DeviceIdType.MESH)

    def greet_mate(i, _):
        greet(at(z, (c + i) % STRIPS))
        return 0

    lax.fori_loop(1, STRIPS, greet_mate, 0)

    def greet_before(i, _):
        greet((((z + NZ - 1) % NZ) * NX_DEV + NX_DEV - 1, i))
        return 0

    lax.fori_loop(0, NS, greet_before, 0)

    def greet_three(plane):
        greet(at(plane, c_lo))
        greet(at(plane, c))
        greet(at(plane, c_hi))

    @pl.when(z == 0)
    def _():
        for j in range(1, 4):
            greet_three(j)

    @pl.when(z > 0)
    def _():
        greet_three(0)

    def greet_upper(j, _):
        greet_three(j)
        return 0

    lax.fori_loop(4, jnp.maximum(z, 4), greet_upper, 0)

    load_guess = pltpu.make_async_copy(guess, gb, ld.at[0])
    load_guess.start()
    load_amp = pltpu.make_async_copy(strengths, amp, ld.at[3])
    load_amp.start()
    for which, field in enumerate((rate, velx, vely, source)):

        @pl.when(x == which)
        def _(field=field):
            pltpu.make_async_copy(field, fb, ld.at[1]).start()

    @pl.when(jnp.logical_and(last_x, z == NZ - 1))
    def _():
        pltpu.make_async_copy(initial, ib, ld.at[2]).start()

    @pl.when(jnp.logical_and(last_x, z < NZ - 1))
    def _():
        pltpu.make_async_copy(guess.at[1], ib, ld.at[2]).start()

    load_guess.wait()
    load_amp.wait()
    pltpu.make_async_copy(rate, fb, ld.at[1]).wait()

    lane8 = lane_ids(8)

    def windows(tile_of, put):
        low = [pltpu.roll(tile_of(k), 32, 1) for k in range(16)]
        for k in range(16):
            put(2 * k, jnp.where(lane8 < 32, low[k - 1], low[k]))
        high = [pltpu.roll(tile_of(k), 96, 1) for k in range(16)]
        for k in range(16):
            put(2 * k + 1, jnp.where(lane8 < 96, high[k], high[(k + 1) % 16]))

    for i in range(2):

        def put_guess(strip, value, i=i):
            for m in range(M):
                value = jnp.where(lane8 == m, amp[M * i + m], value)
            sb[strip, i] = value

        windows(lambda k, i=i: gb[i, :, LANES * k : LANES * (k + 1)], put_guess)

    def put_field(strip, value):
        sb[strip, 2] = value

    windows(lambda k: fb[:, LANES * k : LANES * (k + 1)], put_field)

    @pl.when(last_x)
    def _():
        pltpu.make_async_copy(initial, ib, ld.at[2]).wait()

        def put_before(strip, value):
            sp[strip] = value

        windows(lambda k: ib[:, LANES * k : LANES * (k + 1)], put_before)

    fan = jnp.where(z == 0, NZ - 1, jnp.where(z < 4, 1, NZ - 1 - z))
    pl.semaphore_wait(
        barrier, STRIPS - 1 + jnp.where(last_x, STRIPS, 0) + 3 * fan
    )

    mine = rb.at[pl.ds(3 * x, 3), pl.ds(8 * s, 8)]

    @pl.when(last_x)
    def _():
        def send_before(i, _):
            strip = (c + i) % STRIPS
            pltpu.make_async_remote_copy(
                sp.at[strip], pb.at[pl.ds(8 * s, 8)], sq, rq, at(zn, strip), pl.DeviceIdType.MESH
            ).start()
            return 0

        lax.fori_loop(0, STRIPS, send_before, 0)

    def send_mate(i, _):
        strip = (c + i) % STRIPS
        pltpu.make_async_remote_copy(
            sb.at[strip], mine, s1, r1, at(z, strip), pl.DeviceIdType.MESH
        ).start()
        return 0

    lax.fori_loop(1, STRIPS, send_mate, 0)
    pltpu.make_async_copy(sb.at[c], mine, r1).start()
    pltpu.make_async_copy(rb, rb, r1).wait()

    d, a, b = rb[2], rb[5], rb[8]
    row = lax.broadcasted_iota(jnp.int32, (64, LANES), 0)
    col = lax.broadcasted_iota(jnp.int32, (64, LANES), 1) + (64 * c - 32)
    zero = jnp.zeros((64, LANES), jnp.float32)
    c_mid = 1.0 - (4.0 * d + (jnp.abs(a) + jnp.abs(b)))
    c_xm = jnp.where(row == 0, zero, d + jnp.maximum(a, 0.0))
    c_xp = jnp.where(row == 63, zero, d - jnp.minimum(a, 0.0))
    c_ym = jnp.where(col == 0, zero, d + jnp.maximum(b, 0.0))
    c_yp = jnp.where(col == 2047, zero, d - jnp.minimum(b, 0.0))
    cf[0], cf[1], cf[2], cf[3], cf[4] = c_mid, c_xm, c_xp, c_ym, c_yp
    cf[5] = 1.0 - float(M) * (4.0 * d + (jnp.abs(a) + jnp.abs(b)))
    cf[6], cf[7], cf[8], cf[9] = M * c_xm, M * c_xp, M * c_ym, M * c_yp
    for k in range(5):
        cf[10 + k] = lanes(cf[5 + k], 1)
        cf[15 + k] = lanes(cf[5 + k], -1)

    pltpu.make_async_copy(pb, pb, rq).wait()

    def forced(u, tile, m):
        strength = jnp.broadcast_to(rb[tile, 0:8, m : m + 1], (8, LANES))
        push = rb[11].reshape(8, 8, LANES) * strength[None]
        return stencil(cf, 0, u) + push.reshape(64, LANES)

    tiles = [3 * (k // 2) + k % 2 for k in range(8)]
    state = [pb[...]] + [rb[tile] for tile in tiles[:-1]]
    for m in range(M):
        state = [forced(u, tile, m) for u, tile in zip(state, tiles)]
    for k in range(8):
        rx[k] = state[k]
    state = [u - rb[tile] for u, tile in zip(state, tiles)]
    for m in range(M):
        state = [stencil(cf, 0, u) for u in state]
    for k in range(8):
        rd[k] = state[k]

    entry = jnp.where(z == 0, rx[0] - rx[0], zero)
    local_last = entry
    for k in range(0, 8, 2):
        local_last = coarse_two(cf, local_last, rd[k], rd[k + 1])[1]
    pack_halves(local_last, pk)

    def send_main(packed, plane, slot, sem):
        pltpu.make_async_remote_copy(
            packed, lr.at[slot, pl.ds(1, 2)], s2.at[sem], r2.at[slot], at(plane, c), pl.DeviceIdType.MESH
        ).start()

    def send_sides(packed, plane, slot, sem):
        for src, part, strip in ((packed.at[0], 3, c_lo), (packed.at[1], 0, c_hi)):
            pltpu.make_async_remote_copy(
                src, lr.at[slot, part], s2.at[sem], r2.at[slot], at(plane, strip), pl.DeviceIdType.MESH
            ).start()

    def send_three(packed, plane, slot, sem):
        send_main(packed, plane, slot, sem)
        send_sides(packed, plane, slot, sem)

    def arrived(slot):
        pltpu.make_async_copy(lr.at[slot], lr.at[slot], r2.at[slot]).wait()
        return unpack_window([lr[slot, h] for h in range(4)])

    @pl.when(z == 0)
    def _():
        send_sides(pk, 0, 0, 0)
        pltpu.make_async_copy(pk, lr.at[0, pl.ds(1, 2)], r2.at[0]).start()
        send_three(pk, 1, 0, 1)
        e = arrived(0)
        for j in range(1, 4):
            e = coarse_eight(cf, e) + arrived(j)
            if j == 3:
                pack_halves(e, pe.at[3])
                for plane in (7, 6, 5, 4):
                    send_three(pe.at[3], plane, 0, plane)
            else:
                pack_halves(e, pe.at[j])
        for plane in (3, 2):
            send_three(pe.at[plane - 1], plane, 0, plane)
        eb[...] = entry

    @pl.when(jnp.logical_and(z >= 1, z <= 3))
    def _():
        send_three(pk, 0, z, 1)

    for plane in (7, 6, 5):

        @pl.when(jnp.logical_and(z >= 4, z < plane))
        def _(plane=plane):
            send_three(pk, plane, z - 3, plane)

    for j in range(4, 7):

        @pl.when(z > j)
        def _(j=j):
            ul[j - 4] = arrived(j - 3)

    @pl.when(z >= 1)
    def _():
        eb[...] = lax.fori_loop(0, jnp.maximum(z - 4, 0), lambda j, e: coarse_eight(cf, e) + ul[j], arrived(0))

    lane64 = lane_ids(64)
    err = eb[...]
    for xx in range(NX_DEV):
        first = rx[2 * xx] + err
        mid, err = coarse_two(cf, err, rd[2 * xx], rd[2 * xx + 1])
        second = rx[2 * xx + 1] + mid
        po[xx] = jnp.where(lane64 < 64, pltpu.roll(first, 96, 1), pltpu.roll(second, 32, 1))

        def send_out(i, _, xx=xx):
            ss = (s + i) % NS
            rows = po.at[xx, pl.ds(8 * ss, 8)]
            own = jnp.logical_and(xx == x, i == 0)

            @pl.when(own)
            def _():
                pltpu.make_async_copy(rows, ob.at[c], r3).start()

            @pl.when(jnp.logical_not(own))
            def _():
                pltpu.make_async_remote_copy(
                    rows, ob.at[c], s3, r3, (z * NX_DEV + xx, ss), pl.DeviceIdType.MESH
                ).start()

            return 0

        lax.fori_loop(0, NS, send_out, 0)

    pltpu.make_async_copy(ob, ob, r3).wait()

    sent = sb.at[pl.ds(0, STRIPS - 1)]
    pltpu.make_async_copy(sent, sent, s1).wait()

    @pl.when(last_x)
    def _():
        pltpu.make_async_copy(sp, sp, sq).wait()

    @pl.when(z == 0)
    def _():
        pltpu.make_async_copy(pk, pk, s2.at[0]).wait()
        for plane in range(1, NZ):
            pltpu.make_async_copy(lr.at[0], lr.at[0], s2.at[plane]).wait()

    @pl.when(jnp.logical_and(z >= 1, z <= 3))
    def _():
        pltpu.make_async_copy(lr.at[0], lr.at[0], s2.at[1]).wait()

    for plane in (7, 6, 5):

        @pl.when(jnp.logical_and(z >= 4, z < plane))
        def _(plane=plane):
            pltpu.make_async_copy(lr.at[0], lr.at[0], s2.at[plane]).wait()

    gone = ob.at[pl.ds(0, STRIPS - 1)]
    pltpu.make_async_copy(gone, gone, s3).wait()


def place_rows(ob, out):
    lane8 = lane_ids(8)
    for p in range(16):
        left, right = ob[2 * p], ob[2 * p + 1]
        here = slice(LANES * p, LANES * (p + 1))
        out[0, :, here] = jnp.where(lane8 < 64, left, pltpu.roll(right, 64, 1))
        out[1, :, here] = jnp.where(lane8 < 64, pltpu.roll(left, 64, 1), right)


def per_device(*blocks):
    any_space = pl.BlockSpec(memory_space=pl.ANY)
    f32 = functools.partial(pltpu.VMEM, dtype=jnp.float32)
    sem = pltpu.SemaphoreType.DMA
    strips = pl.pallas_call(
        kernel,
        out_shape=jax.ShapeDtypeStruct((STRIPS, 8, LANES), jnp.float32),
        in_specs=[any_space] * 7,
        out_specs=any_space,
        scratch_shapes=[
            pltpu.SMEM((8,), jnp.float32),
            f32((2, 8, 2048)),
            f32((8, 2048)),
            f32((8, 2048)),
            f32((STRIPS, 3, 8, LANES)),
            f32((STRIPS, 8, LANES)),
            f32((12, 64, LANES)),
            f32((64, LANES)),
            f32((20, 64, LANES)),
            f32((8, 64, LANES)),
            f32((8, 64, LANES)),
            f32((64, LANES)),
            f32((2, 16, LANES)),
            f32((4, 2, 16, LANES)),
            f32((4, 4, 16, LANES)),
            f32((3, 64, LANES)),
            f32((NX_DEV, 64, LANES)),
            sem((4,)),
            sem,
            sem,
            sem,
            sem,
            sem((8,)),
            sem((4,)),
            sem,
            sem,
        ],
        compiler_params=pltpu.CompilerParams(
            collective_id=0, has_side_effects=True, vmem_limit_bytes=56 * 1024 * 1024
        ),
        cost_estimate=pl.CostEstimate(flops=20_000_000, bytes_accessed=700_000, transcendentals=0),
        name="cycle",
    )(*blocks)
    in_vmem = pl.BlockSpec(memory_space=pltpu.VMEM)
    return pl.pallas_call(
        place_rows,
        out_shape=jax.ShapeDtypeStruct((2, 8, 2048), jnp.float32),
        in_specs=[in_vmem],
        out_specs=in_vmem,
        name="place",
    )(strips)


def solution(mesh):
    in_specs = (
        P("space", None),
        P("space", None),
        P("space", None),
        P("space", None),
        P("space", None),
        P("tm"),
        P("tm", "space", None),
    )
    out_specs = P("tm", "space", None)
    return jax.shard_map(
        per_device, mesh=mesh, in_specs=in_specs, out_specs=out_specs, check_vma=False
    )
```

```python
import functools

import jax
import jax.numpy as jnp
from jax import lax
from jax.experimental import pallas as pl
from jax.experimental.pallas import tpu as pltpu
from jax.sharding import PartitionSpec as P

M = 4
NZ = 8
NX_DEV = 4
NS = 8
STRIPS = 32
LANES = 128


def place_of(strip):
    chip, core = strip // 2, strip % 2
    y, q = chip // 4, chip % 4
    x = q + (y % 2) * (3 - 2 * q)
    return x, 2 * y + core


def strip_of(x, s):
    y, core = s // 2, s % 2
    q = x + (y % 2) * (3 - 2 * x)
    return 2 * (4 * y + q) + core


def lane_ids(rows):
    return lax.broadcasted_iota(jnp.int32, (rows, LANES), 1)


def pack_halves(value, out_ref):
    lane = lane_ids(16)
    for half in range(2):
        block = 1 + half
        packed = None
        for group in range(4):
            piece = value[16 * group : 16 * group + 16]
            shift = (32 * (group - block)) % LANES
            moved = piece if shift == 0 else pltpu.roll(piece, shift, 1)
            packed = moved if packed is None else jnp.where(lane < 32 * group, packed, moved)
        out_ref[half] = packed


def unpack_window(parts):
    lane = lane_ids(16)
    rows = []
    for group in range(4):
        row = None
        for block in range(4):
            shift = (32 * (block - group)) % LANES
            moved = parts[block] if shift == 0 else pltpu.roll(parts[block], shift, 1)
            row = moved if row is None else jnp.where(lane < 32 * block, row, moved)
        rows.append(row)
    return jnp.concatenate(rows, axis=0)


def point(cf, base, mid, left, right):
    near = cf[base] * mid + cf[base + 1] * pltpu.roll(mid, 1, 0) + cf[base + 2] * pltpu.roll(mid, 63, 0)
    return near + (cf[base + 3] * left + cf[base + 4] * right)


def lanes(u, steps):
    return pltpu.roll(u, steps % LANES, 1)


def stencil(cf, base, u):
    return point(cf, base, u, lanes(u, 1), lanes(u, -1))


def coarse_two(cf, u, r1=None, r2=None):
    left, left2, right, right2 = lanes(u, 1), lanes(u, 2), lanes(u, -1), lanes(u, -2)
    v = point(cf, 5, u, left, right)
    v_left = point(cf, 10, left, left2, u)
    v_right = point(cf, 15, right, u, right2)
    if r1 is not None:
        v, v_left, v_right = v + r1, v_left + lanes(r1, 1), v_right + lanes(r1, -1)
    w = point(cf, 5, v, v_left, v_right)
    if r2 is not None:
        w = w + r2
    return v, w


def coarse_eight(cf, u):
    def body(i, u):
        for _ in range(2):
            u = coarse_two(cf, u)[1]
        return u

    return lax.fori_loop(0, 2, body, u)


def kernel(
    initial, source, rate, velx, vely, strengths, guess, ob,
    amp, gb, fb, ib, sb, sp, rb, pb, cf, rx, rd, pk, pe, lr, ul, lw, e_in, po,
    ld, s1, r1, sq, rq, s2, r2, r4, s3, r3, ready,
):
    t, s = lax.axis_index("tm"), lax.axis_index("space")
    z, x = t // NX_DEV, t % NX_DEV
    c = strip_of(x, s)
    c_lo, c_hi = (c + STRIPS - 1) % STRIPS, (c + 1) % STRIPS
    gives_next = jnp.logical_and(x == NX_DEV - 1, z < NZ - 1)
    gives_first = jnp.logical_and(x == 0, z == 0)
    gives = jnp.logical_or(gives_next, gives_first)

    def at(plane, strip):
        px, ps = place_of(strip)
        return (plane * NX_DEV + px, ps)

    barrier = pltpu.get_barrier_semaphore()

    def greet(device):
        pl.semaphore_signal(barrier, inc=1, device_id=device, device_id_type=pl.DeviceIdType.MESH)

    def greet_mate(i, _):
        greet(at(z, (c + i) % STRIPS))
        return 0

    lax.fori_loop(1, STRIPS, greet_mate, 0)

    def greet_before(i, _):
        greet(((z - 1) * NX_DEV + NX_DEV - 1, i))
        return 0

    lax.fori_loop(0, jnp.where(z > 0, NS, 0), greet_before, 0)

    def greet_three(plane):
        greet(at(plane, c_lo))
        greet(at(plane, c))
        greet(at(plane, c_hi))

    @pl.when(z == 0)
    def _():
        for plane in range(1, 4):
            greet(at(plane, c))
        for plane in range(4, NZ):
            greet_three(plane)

    def greet_upper(plane, _):
        greet(at(plane, c))
        return 0

    lax.fori_loop(4, jnp.maximum(z, 4), greet_upper, 0)

    @pl.when(z == 7)
    def _():
        greet(at(4, c_lo))
        greet(at(4, c_hi))

    load_guess = pltpu.make_async_copy(guess, gb, ld.at[0])
    load_guess.start()
    load_amp = pltpu.make_async_copy(strengths, amp, ld.at[3])
    load_amp.start()
    for which, field in enumerate((rate, velx, vely, source)):

        @pl.when(x == which)
        def _(field=field):
            pltpu.make_async_copy(field, fb, ld.at[1]).start()

    @pl.when(gives_first)
    def _():
        pltpu.make_async_copy(initial, ib, ld.at[2]).start()

    @pl.when(gives_next)
    def _():
        pltpu.make_async_copy(guess.at[1], ib, ld.at[2]).start()

    load_guess.wait()
    load_amp.wait()
    pltpu.make_async_copy(rate, fb, ld.at[1]).wait()

    lane8 = lane_ids(8)

    def windows(tile_of, put):
        low = [pltpu.roll(tile_of(k), 32, 1) for k in range(16)]
        for k in range(16):
            put(2 * k, jnp.where(lane8 < 32, low[k - 1], low[k]))
        high = [pltpu.roll(tile_of(k), 96, 1) for k in range(16)]
        for k in range(16):
            put(2 * k + 1, jnp.where(lane8 < 96, high[k], high[(k + 1) % 16]))

    for i in range(2):

        def put_guess(strip, value, i=i):
            for m in range(M):
                value = jnp.where(lane8 == m, amp[M * i + m], value)
            sb[strip, i] = value

        windows(lambda k, i=i: gb[i, :, LANES * k : LANES * (k + 1)], put_guess)

    def put_field(strip, value):
        sb[strip, 2] = value

    windows(lambda k: fb[:, LANES * k : LANES * (k + 1)], put_field)

    @pl.when(gives)
    def _():
        pltpu.make_async_copy(initial, ib, ld.at[2]).wait()

        def put_before(strip, value):
            sp[strip] = value

        windows(lambda k: ib[:, LANES * k : LANES * (k + 1)], put_before)

    hubs = jnp.where(z == 0, 0, jnp.where(z < 4, 1, 3))
    uppers = jnp.where(z == 4, 5, jnp.where(z == 5, 2, jnp.where(z == 6, 1, 0)))
    pl.semaphore_wait(barrier, STRIPS - 1 + jnp.where(gives_next, STRIPS, 0) + hubs + uppers)

    def signal_ready(strip):
        pl.semaphore_signal(
            ready.at[z], inc=1, device_id=at(0, strip), device_id_type=pl.DeviceIdType.MESH
        )

    @pl.when(z > 0)
    def _():
        signal_ready(c)

    @pl.when(z >= 4)
    def _():
        signal_ready(c_lo)
        signal_ready(c_hi)

    mine = rb.at[pl.ds(3 * x, 3), pl.ds(8 * s, 8)]

    ahead = pb.at[pl.ds(8 * s, 8)]

    @pl.when(gives)
    def _():
        to = jnp.where(gives_next, z + 1, 0)

        def send_before(i, _):
            strip = (c + i) % STRIPS
            pltpu.make_async_remote_copy(
                sp.at[strip], ahead, sq, rq, at(to, strip), pl.DeviceIdType.MESH
            ).start()
            return 0

        lax.fori_loop(jnp.where(gives_next, 0, 1), STRIPS, send_before, 0)

        @pl.when(gives_first)
        def _():
            pltpu.make_async_copy(sp.at[c], ahead, rq).start()

    def send_mate(i, _):
        strip = (c + i) % STRIPS
        pltpu.make_async_remote_copy(
            sb.at[strip], mine, s1, r1, at(z, strip), pl.DeviceIdType.MESH
        ).start()
        return 0

    lax.fori_loop(1, STRIPS, send_mate, 0)
    pltpu.make_async_copy(sb.at[c], mine, r1).start()
    pltpu.make_async_copy(rb, rb, r1).wait()

    d, a, b = rb[2], rb[5], rb[8]
    row = lax.broadcasted_iota(jnp.int32, (64, LANES), 0)
    col = lax.broadcasted_iota(jnp.int32, (64, LANES), 1) + (64 * c - 32)
    zero = jnp.zeros((64, LANES), jnp.float32)
    c_mid = 1.0 - (4.0 * d + (jnp.abs(a) + jnp.abs(b)))
    c_xm = jnp.where(row == 0, zero, d + jnp.maximum(a, 0.0))
    c_xp = jnp.where(row == 63, zero, d - jnp.minimum(a, 0.0))
    c_ym = jnp.where(col == 0, zero, d + jnp.maximum(b, 0.0))
    c_yp = jnp.where(col == 2047, zero, d - jnp.minimum(b, 0.0))
    cf[0], cf[1], cf[2], cf[3], cf[4] = c_mid, c_xm, c_xp, c_ym, c_yp
    cf[5] = 1.0 - float(M) * (4.0 * d + (jnp.abs(a) + jnp.abs(b)))
    cf[6], cf[7], cf[8], cf[9] = M * c_xm, M * c_xp, M * c_ym, M * c_yp
    for k in range(5):
        cf[10 + k] = lanes(cf[5 + k], 1)
        cf[15 + k] = lanes(cf[5 + k], -1)

    pltpu.make_async_copy(pb, pb, rq).wait()

    def forced(u, tile, m):
        strength = jnp.broadcast_to(rb[tile, 0:8, m : m + 1], (8, LANES))
        push = rb[11].reshape(8, 8, LANES) * strength[None]
        return stencil(cf, 0, u) + push.reshape(64, LANES)

    tiles = [3 * (k // 2) + k % 2 for k in range(8)]
    state = [pb[...]] + [rb[tile] for tile in tiles[:-1]]
    for m in range(M):
        state = [forced(u, tile, m) for u, tile in zip(state, tiles)]
    for k in range(8):
        rx[k] = state[k]
    state = [u - rb[tile] for u, tile in zip(state, tiles)]
    for m in range(M):
        state = [stencil(cf, 0, u) for u in state]
    for k in range(8):
        rd[k] = state[k]

    entry = jnp.where(z == 0, rx[0] - rx[0], zero)
    def send_main(packed, plane, slot, sem):
        pltpu.make_async_remote_copy(
            packed, lr.at[slot, pl.ds(1, 2)], s2.at[sem], r2.at[slot], at(plane, c), pl.DeviceIdType.MESH
        ).start()

    def send_sides(packed, plane, slot, sem):
        for src, part, strip in ((packed.at[0], 3, c_lo), (packed.at[1], 0, c_hi)):
            pltpu.make_async_remote_copy(
                src, lr.at[slot, part], s2.at[sem], r2.at[slot], at(plane, strip), pl.DeviceIdType.MESH
            ).start()

    def send_three(packed, plane, slot, sem):
        send_main(packed, plane, slot, sem)
        send_sides(packed, plane, slot, sem)

    def send_window(window, plane, slot, sem):
        pltpu.make_async_remote_copy(
            window, ul.at[slot], s2.at[sem], r4.at[slot], at(plane, c), pl.DeviceIdType.MESH
        ).start()

    def window_arrived(slot):
        pltpu.make_async_copy(ul.at[slot], ul.at[slot], r4.at[slot]).wait()

    def arrived(slot):
        pltpu.make_async_copy(lr.at[slot], lr.at[slot], r2.at[slot]).wait()
        return unpack_window([lr[slot, h] for h in range(4)])

    lane64 = lane_ids(64)

    def chain(err):
        for xx in range(NX_DEV):
            first = rx[2 * xx] + err
            mid, err = coarse_two(cf, err, rd[2 * xx], rd[2 * xx + 1])
            second = rx[2 * xx + 1] + mid
            po[xx] = jnp.where(lane64 < 64, pltpu.roll(first, 96, 1), pltpu.roll(second, 32, 1))
        return err

    def send_out(i, _):
        xx, ss = (x + i // NS) % NX_DEV, (s + i) % NS
        pltpu.make_async_remote_copy(
            po.at[xx, pl.ds(8 * ss, 8)], ob.at[c], s3, r3, (z * NX_DEV + xx, ss), pl.DeviceIdType.MESH
        ).start()
        return 0

    def send_results():
        lax.fori_loop(1, STRIPS, send_out, 0)
        pltpu.make_async_copy(po.at[x, pl.ds(8 * s, 8)], ob.at[c], r3).start()

    @pl.when(z == 0)
    def _():
        e = chain(entry)
        lw[0] = e
        pack_halves(e, pk)
        send_sides(pk, 0, 0, 0)
        pltpu.make_async_copy(pk, lr.at[0, pl.ds(1, 2)], r2.at[0]).start()
        pl.semaphore_wait(ready.at[1], 1)
        send_window(lw.at[0], 1, 0, 1)
        send_results()
        e = arrived(0)
        for j in range(1, 4):
            e = coarse_eight(cf, e)
            window_arrived(j - 1)
            e = e + ul[j - 1]
            if j < 3:
                lw[j] = e
                pl.semaphore_wait(ready.at[j + 1], 1)
                send_window(lw.at[j], j + 1, 0, j + 1)
        pack_halves(e, pe)
        for plane in (7, 6, 5, 4):
            pl.semaphore_wait(ready.at[plane], 3)
            send_three(pe, plane, 0, plane)

    @pl.when(z > 0)
    def _():
        local_last = zero
        for k in range(0, 8, 2):
            local_last = coarse_two(cf, local_last, rd[k], rd[k + 1])[1]
        lw[0] = local_last

    @pl.when(jnp.logical_and(z >= 1, z <= 3))
    def _():
        send_window(lw.at[0], 0, z - 1, 1)

    @pl.when(z == 4)
    def _():
        pack_halves(lw[0], pk)
        send_three(pk, 7, 1, 7)

    for plane in (7, 6, 5):

        @pl.when(jnp.logical_and(z >= (5 if plane == 7 else 4), z < plane))
        def _(plane=plane):
            send_window(lw.at[0], plane, z - 4, plane)

    for j in range(4, 7):

        @pl.when(jnp.logical_and(z > j, z < 7) if j == 4 else z > j)
        def _(j=j):
            window_arrived(j - 4)

    @pl.when(z == 7)
    def _():
        ul[0] = arrived(1)

    @pl.when(jnp.logical_and(z >= 1, z <= 3))
    def _():
        window_arrived(0)
        e_in[...] = ul[0]

    @pl.when(z >= 4)
    def _():
        e_in[...] = lax.fori_loop(
            0, jnp.maximum(z - 4, 0), lambda j, e: coarse_eight(cf, e) + ul[j], arrived(0)
        )

    @pl.when(z > 0)
    def _():
        chain(e_in[...])
        send_results()

    pltpu.make_async_copy(ob, ob, r3).wait()

    sent = sb.at[pl.ds(0, STRIPS - 1)]
    pltpu.make_async_copy(sent, sent, s1).wait()

    @pl.when(gives_next)
    def _():
        pltpu.make_async_copy(sp, sp, sq).wait()

    @pl.when(gives_first)
    def _():
        most = sp.at[pl.ds(0, STRIPS - 1)]
        pltpu.make_async_copy(most, most, sq).wait()

    @pl.when(z == 0)
    def _():
        pltpu.make_async_copy(pk, pk, s2.at[0]).wait()
        for plane in range(1, NZ):
            pltpu.make_async_copy(lr.at[0], lr.at[0], s2.at[plane]).wait()

    @pl.when(jnp.logical_and(z >= 1, z <= 3))
    def _():
        pltpu.make_async_copy(lr.at[0], lr.at[0], s2.at[1]).wait()

    for plane in (7, 6, 5):

        @pl.when(jnp.logical_and(z >= 4, z < plane))
        def _(plane=plane):
            pltpu.make_async_copy(lr.at[0], lr.at[0], s2.at[plane]).wait()

    gone = ob.at[pl.ds(0, STRIPS - 1)]
    pltpu.make_async_copy(gone, gone, s3).wait()


def place_rows(ob, out):
    lane8 = lane_ids(8)
    for p in range(16):
        left, right = ob[2 * p], ob[2 * p + 1]
        here = slice(LANES * p, LANES * (p + 1))
        out[0, :, here] = jnp.where(lane8 < 64, left, pltpu.roll(right, 64, 1))
        out[1, :, here] = jnp.where(lane8 < 64, pltpu.roll(left, 64, 1), right)


def per_device(*blocks):
    any_space = pl.BlockSpec(memory_space=pl.ANY)
    f32 = functools.partial(pltpu.VMEM, dtype=jnp.float32)
    sem = pltpu.SemaphoreType.DMA
    strips = pl.pallas_call(
        kernel,
        out_shape=jax.ShapeDtypeStruct((STRIPS, 8, LANES), jnp.float32),
        in_specs=[any_space] * 7,
        out_specs=any_space,
        scratch_shapes=[
            pltpu.SMEM((8,), jnp.float32),
            f32((2, 8, 2048)),
            f32((8, 2048)),
            f32((8, 2048)),
            f32((STRIPS, 3, 8, LANES)),
            f32((STRIPS, 8, LANES)),
            f32((12, 64, LANES)),
            f32((64, LANES)),
            f32((20, 64, LANES)),
            f32((8, 64, LANES)),
            f32((8, 64, LANES)),
            f32((2, 16, LANES)),
            f32((2, 16, LANES)),
            f32((2, 4, 16, LANES)),
            f32((3, 64, LANES)),
            f32((3, 64, LANES)),
            f32((64, LANES)),
            f32((NX_DEV, 64, LANES)),
            sem((4,)),
            sem,
            sem,
            sem,
            sem,
            sem((8,)),
            sem((2,)),
            sem((3,)),
            sem,
            sem,
            pltpu.SemaphoreType.REGULAR((NZ,)),
        ],
        compiler_params=pltpu.CompilerParams(
            collective_id=0, has_side_effects=True, vmem_limit_bytes=56 * 1024 * 1024
        ),
        cost_estimate=pl.CostEstimate(flops=20_000_000, bytes_accessed=700_000, transcendentals=0),
        name="cycle",
    )(*blocks)
    in_vmem = pl.BlockSpec(memory_space=pltpu.VMEM)
    return pl.pallas_call(
        place_rows,
        out_shape=jax.ShapeDtypeStruct((2, 8, 2048), jnp.float32),
        in_specs=[in_vmem],
        out_specs=in_vmem,
        name="place",
    )(strips)


def solution(mesh):
    in_specs = (
        P("space", None),
        P("space", None),
        P("space", None),
        P("space", None),
        P("space", None),
        P("tm"),
        P("tm", "space", None),
    )
    out_specs = P("tm", "space", None)
    return jax.shard_map(
        per_device, mesh=mesh, in_specs=in_specs, out_specs=out_specs, check_vma=False
    )
```

```python
import functools

import jax
import jax.numpy as jnp
from jax import lax
from jax.experimental import pallas as pl
from jax.experimental.pallas import tpu as pltpu
from jax.sharding import PartitionSpec as P

M = 4
NZ = 8
NX_DEV = 4
NS = 8
STRIPS = 32
LANES = 128


OFFSETS = sorted(
    ((dx, dy, dc) for dx in range(4) for dy in range(4) for dc in range(2)),
    key=lambda o: (-min(o[0], 4 - o[0]) - min(o[1], 4 - o[1]), -o[2]),
)


def place_of(strip):
    chip, core = strip // 2, strip % 2
    y, q = chip // 4, chip % 4
    x = q + (y % 2) * (3 - 2 * q)
    return x, 2 * y + core


def strip_of(x, s):
    y, core = s // 2, s % 2
    q = x + (y % 2) * (3 - 2 * x)
    return 2 * (4 * y + q) + core


def lane_ids(rows):
    return lax.broadcasted_iota(jnp.int32, (rows, LANES), 1)


def pack_halves(value, out_ref):
    lane = lane_ids(16)
    for half in range(2):
        block = 1 + half
        packed = None
        for group in range(4):
            piece = value[16 * group : 16 * group + 16]
            shift = (32 * (group - block)) % LANES
            moved = piece if shift == 0 else pltpu.roll(piece, shift, 1)
            packed = moved if packed is None else jnp.where(lane < 32 * group, packed, moved)
        out_ref[half] = packed


def unpack_window(parts):
    lane = lane_ids(16)
    rows = []
    for group in range(4):
        row = None
        for block in range(4):
            shift = (32 * (block - group)) % LANES
            moved = parts[block] if shift == 0 else pltpu.roll(parts[block], shift, 1)
            row = moved if row is None else jnp.where(lane < 32 * block, row, moved)
        rows.append(row)
    return jnp.concatenate(rows, axis=0)


def point(cf, base, mid, left, right):
    near = cf[base] * mid + cf[base + 1] * pltpu.roll(mid, 1, 0) + cf[base + 2] * pltpu.roll(mid, 63, 0)
    return near + (cf[base + 3] * left + cf[base + 4] * right)


def lanes(u, steps):
    return pltpu.roll(u, steps % LANES, 1)


def stencil(cf, base, u):
    return point(cf, base, u, lanes(u, 1), lanes(u, -1))


def coarse_two(cf, u, r1=None, r2=None):
    left, left2, right, right2 = lanes(u, 1), lanes(u, 2), lanes(u, -1), lanes(u, -2)
    v = point(cf, 5, u, left, right)
    v_left = point(cf, 10, left, left2, u)
    v_right = point(cf, 15, right, u, right2)
    if r1 is not None:
        v, v_left, v_right = v + r1, v_left + lanes(r1, 1), v_right + lanes(r1, -1)
    w = point(cf, 5, v, v_left, v_right)
    if r2 is not None:
        w = w + r2
    return v, w


def coarse_eight(cf, u):
    def body(i, u):
        for _ in range(2):
            u = coarse_two(cf, u)[1]
        return u

    return lax.fori_loop(0, 2, body, u)


def kernel(
    initial, source, rate, velx, vely, strengths, guess, ob,
    amp, gb, fb, ib, sb, sp, rb, pb, cf, rx, rd, pk, pe, lr, ul, lw, e_in, po,
    ld, s1, r1, sq, rq, s2, r2, r4, s3, r3, ready,
):
    t, s = lax.axis_index("tm"), lax.axis_index("space")
    z, x = t // NX_DEV, t % NX_DEV
    c = strip_of(x, s)
    c_lo, c_hi = (c + STRIPS - 1) % STRIPS, (c + 1) % STRIPS
    gives_next = jnp.logical_and(x == NX_DEV - 1, z < NZ - 1)
    gives_first = jnp.logical_and(x == 0, z == 0)
    gives = jnp.logical_or(gives_next, gives_first)

    def at(plane, strip):
        px, ps = place_of(strip)
        return (plane * NX_DEV + px, ps)

    barrier = pltpu.get_barrier_semaphore()

    def greet(device):
        pl.semaphore_signal(barrier, inc=1, device_id=device, device_id_type=pl.DeviceIdType.MESH)

    def mate(dx, dy, dc):
        ps = (s + 2 * dy) % NS
        return (x + dx) % NX_DEV, ps if dc == 0 else ps + 1 - 2 * (s % 2)

    for offset in OFFSETS[:-1]:
        px, ps = mate(*offset)
        greet((z * NX_DEV + px, ps))

    def greet_before(i, _):
        greet(((z - 1) * NX_DEV + NX_DEV - 1, i))
        return 0

    lax.fori_loop(0, jnp.where(z > 0, NS, 0), greet_before, 0)

    def greet_three(plane):
        greet(at(plane, c_lo))
        greet(at(plane, c))
        greet(at(plane, c_hi))

    @pl.when(z == 0)
    def _():
        for plane in range(1, 4):
            greet(at(plane, c))
        for plane in range(4, NZ):
            greet_three(plane)

    def greet_upper(plane, _):
        greet(at(plane, c))
        return 0

    lax.fori_loop(4, jnp.maximum(z, 4), greet_upper, 0)

    @pl.when(z == 7)
    def _():
        greet(at(4, c_lo))
        greet(at(4, c_hi))

    load_guess = pltpu.make_async_copy(guess, gb, ld.at[0])
    load_guess.start()
    load_amp = pltpu.make_async_copy(strengths, amp, ld.at[3])
    load_amp.start()
    for which, field in enumerate((rate, velx, vely, source)):

        @pl.when(x == which)
        def _(field=field):
            pltpu.make_async_copy(field, fb, ld.at[1]).start()

    @pl.when(gives_first)
    def _():
        pltpu.make_async_copy(initial, ib, ld.at[2]).start()

    @pl.when(gives_next)
    def _():
        pltpu.make_async_copy(guess.at[1], ib, ld.at[2]).start()

    load_guess.wait()
    load_amp.wait()
    pltpu.make_async_copy(rate, fb, ld.at[1]).wait()

    lane8 = lane_ids(8)

    def windows(tile_of, put):
        low = [pltpu.roll(tile_of(k), 32, 1) for k in range(16)]
        for k in range(16):
            put(2 * k, jnp.where(lane8 < 32, low[k - 1], low[k]))
        high = [pltpu.roll(tile_of(k), 96, 1) for k in range(16)]
        for k in range(16):
            put(2 * k + 1, jnp.where(lane8 < 96, high[k], high[(k + 1) % 16]))

    for i in range(2):

        def put_guess(strip, value, i=i):
            for m in range(M):
                value = jnp.where(lane8 == m, amp[M * i + m], value)
            sb[strip, i] = value

        windows(lambda k, i=i: gb[i, :, LANES * k : LANES * (k + 1)], put_guess)

    def put_field(strip, value):
        sb[strip, 2] = value

    windows(lambda k: fb[:, LANES * k : LANES * (k + 1)], put_field)

    @pl.when(gives)
    def _():
        pltpu.make_async_copy(initial, ib, ld.at[2]).wait()

        def put_before(strip, value):
            sp[strip] = value

        windows(lambda k: ib[:, LANES * k : LANES * (k + 1)], put_before)

    hubs = jnp.where(z == 0, 0, jnp.where(z < 4, 1, 3))
    uppers = jnp.where(z == 4, 5, jnp.where(z == 5, 2, jnp.where(z == 6, 1, 0)))
    pl.semaphore_wait(barrier, STRIPS - 1 + jnp.where(gives_next, STRIPS, 0) + hubs + uppers)

    def signal_ready(strip):
        pl.semaphore_signal(
            ready.at[z], inc=1, device_id=at(0, strip), device_id_type=pl.DeviceIdType.MESH
        )

    @pl.when(z > 0)
    def _():
        signal_ready(c)

    @pl.when(z >= 4)
    def _():
        signal_ready(c_lo)
        signal_ready(c_hi)

    mine = rb.at[pl.ds(3 * x, 3), pl.ds(8 * s, 8)]

    ahead = pb.at[pl.ds(8 * s, 8)]

    @pl.when(gives)
    def _():
        to = jnp.where(gives_next, z + 1, 0)

        def give(offset):
            px, ps = mate(*offset)
            pltpu.make_async_remote_copy(
                sp.at[strip_of(px, ps)], ahead, sq, rq, (to * NX_DEV + px, ps), pl.DeviceIdType.MESH
            ).start()

        for offset in OFFSETS[:-1]:
            give(offset)

        @pl.when(gives_next)
        def _():
            give(OFFSETS[-1])

        @pl.when(gives_first)
        def _():
            pltpu.make_async_copy(sp.at[c], ahead, rq).start()

    for offset in OFFSETS[:-1]:
        px, ps = mate(*offset)
        pltpu.make_async_remote_copy(
            sb.at[strip_of(px, ps)], mine, s1, r1, (z * NX_DEV + px, ps), pl.DeviceIdType.MESH
        ).start()
    pltpu.make_async_copy(sb.at[c], mine, r1).start()
    pltpu.make_async_copy(rb, rb, r1).wait()

    d, a, b = rb[2], rb[5], rb[8]
    row = lax.broadcasted_iota(jnp.int32, (64, LANES), 0)
    col = lax.broadcasted_iota(jnp.int32, (64, LANES), 1) + (64 * c - 32)
    zero = jnp.zeros((64, LANES), jnp.float32)
    c_mid = 1.0 - (4.0 * d + (jnp.abs(a) + jnp.abs(b)))
    c_xm = jnp.where(row == 0, zero, d + jnp.maximum(a, 0.0))
    c_xp = jnp.where(row == 63, zero, d - jnp.minimum(a, 0.0))
    c_ym = jnp.where(col == 0, zero, d + jnp.maximum(b, 0.0))
    c_yp = jnp.where(col == 2047, zero, d - jnp.minimum(b, 0.0))
    cf[0], cf[1], cf[2], cf[3], cf[4] = c_mid, c_xm, c_xp, c_ym, c_yp
    cf[5] = 1.0 - float(M) * (4.0 * d + (jnp.abs(a) + jnp.abs(b)))
    cf[6], cf[7], cf[8], cf[9] = M * c_xm, M * c_xp, M * c_ym, M * c_yp
    for k in range(5):
        cf[10 + k] = lanes(cf[5 + k], 1)
        cf[15 + k] = lanes(cf[5 + k], -1)

    pltpu.make_async_copy(pb, pb, rq).wait()

    def forced(u, tile, m):
        strength = jnp.broadcast_to(rb[tile, 0:8, m : m + 1], (8, LANES))
        push = rb[11].reshape(8, 8, LANES) * strength[None]
        return stencil(cf, 0, u) + push.reshape(64, LANES)

    tiles = [3 * (k // 2) + k % 2 for k in range(8)]
    state = [pb[...]] + [rb[tile] for tile in tiles[:-1]]
    for m in range(M):
        state = [forced(u, tile, m) for u, tile in zip(state, tiles)]
    for k in range(8):
        rx[k] = state[k]
    state = [u - rb[tile] for u, tile in zip(state, tiles)]
    for m in range(M):
        state = [stencil(cf, 0, u) for u in state]
    for k in range(8):
        rd[k] = state[k]

    entry = jnp.where(z == 0, rx[0] - rx[0], zero)
    def send_main(packed, plane, slot, sem):
        pltpu.make_async_remote_copy(
            packed, lr.at[slot, pl.ds(1, 2)], s2.at[sem], r2.at[slot], at(plane, c), pl.DeviceIdType.MESH
        ).start()

    def send_sides(packed, plane, slot, sem):
        for src, part, strip in ((packed.at[0], 3, c_lo), (packed.at[1], 0, c_hi)):
            pltpu.make_async_remote_copy(
                src, lr.at[slot, part], s2.at[sem], r2.at[slot], at(plane, strip), pl.DeviceIdType.MESH
            ).start()

    def send_three(packed, plane, slot, sem):
        send_main(packed, plane, slot, sem)
        send_sides(packed, plane, slot, sem)

    def send_window(window, plane, slot, sem):
        pltpu.make_async_remote_copy(
            window, ul.at[slot], s2.at[sem], r4.at[slot], at(plane, c), pl.DeviceIdType.MESH
        ).start()

    def window_arrived(slot):
        pltpu.make_async_copy(ul.at[slot], ul.at[slot], r4.at[slot]).wait()

    def arrived(slot):
        pltpu.make_async_copy(lr.at[slot], lr.at[slot], r2.at[slot]).wait()
        return unpack_window([lr[slot, h] for h in range(4)])

    lane64 = lane_ids(64)

    def chain(err):
        for xx in range(NX_DEV):
            first = rx[2 * xx] + err
            mid, err = coarse_two(cf, err, rd[2 * xx], rd[2 * xx + 1])
            second = rx[2 * xx + 1] + mid
            po[xx] = jnp.where(lane64 < 64, pltpu.roll(first, 96, 1), pltpu.roll(second, 32, 1))
        return err

    def send_results():
        for offset in OFFSETS[:-1]:
            px, ps = mate(*offset)
            pltpu.make_async_remote_copy(
                po.at[px, pl.ds(8 * ps, 8)], ob.at[c], s3, r3, (z * NX_DEV + px, ps), pl.DeviceIdType.MESH
            ).start()
        pltpu.make_async_copy(po.at[x, pl.ds(8 * s, 8)], ob.at[c], r3).start()

    @pl.when(z == 0)
    def _():
        e = chain(entry)
        lw[0] = e
        pack_halves(e, pk)
        send_sides(pk, 0, 0, 0)
        pltpu.make_async_copy(pk, lr.at[0, pl.ds(1, 2)], r2.at[0]).start()
        pl.semaphore_wait(ready.at[1], 1)
        send_window(lw.at[0], 1, 0, 1)
        send_results()
        e = arrived(0)
        for j in range(1, 4):
            e = coarse_eight(cf, e)
            window_arrived(j - 1)
            e = e + ul[j - 1]
            if j < 3:
                lw[j] = e
                pl.semaphore_wait(ready.at[j + 1], 1)
                send_window(lw.at[j], j + 1, 0, j + 1)
        pack_halves(e, pe)
        for plane in (7, 6, 5, 4):
            pl.semaphore_wait(ready.at[plane], 3)
            send_three(pe, plane, 0, plane)

    @pl.when(z > 0)
    def _():
        local_last = zero
        for k in range(0, 8, 2):
            local_last = coarse_two(cf, local_last, rd[k], rd[k + 1])[1]
        lw[0] = local_last

    @pl.when(jnp.logical_and(z >= 1, z <= 3))
    def _():
        send_window(lw.at[0], 0, z - 1, 1)

    @pl.when(z == 4)
    def _():
        pack_halves(lw[0], pk)
        send_three(pk, 7, 1, 7)

    for plane in (7, 6, 5):

        @pl.when(jnp.logical_and(z >= (5 if plane == 7 else 4), z < plane))
        def _(plane=plane):
            send_window(lw.at[0], plane, z - 4, plane)

    for j in range(4, 7):

        @pl.when(jnp.logical_and(z > j, z < 7) if j == 4 else z > j)
        def _(j=j):
            window_arrived(j - 4)

    @pl.when(z == 7)
    def _():
        ul[0] = arrived(1)

    @pl.when(jnp.logical_and(z >= 1, z <= 3))
    def _():
        window_arrived(0)
        e_in[...] = ul[0]

    @pl.when(z >= 4)
    def _():
        e_in[...] = lax.fori_loop(
            0, jnp.maximum(z - 4, 0), lambda j, e: coarse_eight(cf, e) + ul[j], arrived(0)
        )

    @pl.when(z > 0)
    def _():
        chain(e_in[...])
        send_results()

    pltpu.make_async_copy(ob, ob, r3).wait()

    sent = sb.at[pl.ds(0, STRIPS - 1)]
    pltpu.make_async_copy(sent, sent, s1).wait()

    @pl.when(gives_next)
    def _():
        pltpu.make_async_copy(sp, sp, sq).wait()

    @pl.when(gives_first)
    def _():
        most = sp.at[pl.ds(0, STRIPS - 1)]
        pltpu.make_async_copy(most, most, sq).wait()

    @pl.when(z == 0)
    def _():
        pltpu.make_async_copy(pk, pk, s2.at[0]).wait()
        for plane in range(1, NZ):
            pltpu.make_async_copy(lr.at[0], lr.at[0], s2.at[plane]).wait()

    @pl.when(jnp.logical_and(z >= 1, z <= 3))
    def _():
        pltpu.make_async_copy(lr.at[0], lr.at[0], s2.at[1]).wait()

    for plane in (7, 6, 5):

        @pl.when(jnp.logical_and(z >= 4, z < plane))
        def _(plane=plane):
            pltpu.make_async_copy(lr.at[0], lr.at[0], s2.at[plane]).wait()

    gone = ob.at[pl.ds(0, STRIPS - 1)]
    pltpu.make_async_copy(gone, gone, s3).wait()


def place_rows(ob, out):
    lane8 = lane_ids(8)
    for p in range(16):
        left, right = ob[2 * p], ob[2 * p + 1]
        here = slice(LANES * p, LANES * (p + 1))
        out[0, :, here] = jnp.where(lane8 < 64, left, pltpu.roll(right, 64, 1))
        out[1, :, here] = jnp.where(lane8 < 64, pltpu.roll(left, 64, 1), right)


def per_device(*blocks):
    any_space = pl.BlockSpec(memory_space=pl.ANY)
    f32 = functools.partial(pltpu.VMEM, dtype=jnp.float32)
    sem = pltpu.SemaphoreType.DMA
    strips = pl.pallas_call(
        kernel,
        out_shape=jax.ShapeDtypeStruct((STRIPS, 8, LANES), jnp.float32),
        in_specs=[any_space] * 7,
        out_specs=any_space,
        scratch_shapes=[
            pltpu.SMEM((8,), jnp.float32),
            f32((2, 8, 2048)),
            f32((8, 2048)),
            f32((8, 2048)),
            f32((STRIPS, 3, 8, LANES)),
            f32((STRIPS, 8, LANES)),
            f32((12, 64, LANES)),
            f32((64, LANES)),
            f32((20, 64, LANES)),
            f32((8, 64, LANES)),
            f32((8, 64, LANES)),
            f32((2, 16, LANES)),
            f32((2, 16, LANES)),
            f32((2, 4, 16, LANES)),
            f32((3, 64, LANES)),
            f32((3, 64, LANES)),
            f32((64, LANES)),
            f32((NX_DEV, 64, LANES)),
            sem((4,)),
            sem,
            sem,
            sem,
            sem,
            sem((8,)),
            sem((2,)),
            sem((3,)),
            sem,
            sem,
            pltpu.SemaphoreType.REGULAR((NZ,)),
        ],
        compiler_params=pltpu.CompilerParams(
            collective_id=0, has_side_effects=True, vmem_limit_bytes=56 * 1024 * 1024
        ),
        cost_estimate=pl.CostEstimate(flops=20_000_000, bytes_accessed=700_000, transcendentals=0),
        name="cycle",
    )(*blocks)
    in_vmem = pl.BlockSpec(memory_space=pltpu.VMEM)
    return pl.pallas_call(
        place_rows,
        out_shape=jax.ShapeDtypeStruct((2, 8, 2048), jnp.float32),
        in_specs=[in_vmem],
        out_specs=in_vmem,
        name="place",
    )(strips)


def solution(mesh):
    in_specs = (
        P("space", None),
        P("space", None),
        P("space", None),
        P("space", None),
        P("space", None),
        P("tm"),
        P("tm", "space", None),
    )
    out_specs = P("tm", "space", None)
    return jax.shard_map(
        per_device, mesh=mesh, in_specs=in_specs, out_specs=out_specs, check_vma=False
    )
```

```python
import functools

import jax
import jax.numpy as jnp
from jax import lax
from jax.experimental import pallas as pl
from jax.experimental.pallas import tpu as pltpu
from jax.sharding import PartitionSpec as P

M = 4
NZ = 8
NX_DEV = 4
NS = 8
STRIPS = 32
LANES = 128


OFFSETS = sorted(
    ((dx, dy, dc) for dx in range(4) for dy in range(4) for dc in range(2)),
    key=lambda o: (-min(o[0], 4 - o[0]) - min(o[1], 4 - o[1]), -o[2]),
)


def place_of(strip):
    chip, core = strip // 2, strip % 2
    y, q = chip // 4, chip % 4
    x = q + (y % 2) * (3 - 2 * q)
    return x, 2 * y + core


def strip_of(x, s):
    y, core = s // 2, s % 2
    q = x + (y % 2) * (3 - 2 * x)
    return 2 * (4 * y + q) + core


def lane_ids(rows):
    return lax.broadcasted_iota(jnp.int32, (rows, LANES), 1)


def pack_halves(value, out_ref):
    lane = lane_ids(16)
    for half in range(2):
        block = 1 + half
        packed = None
        for group in range(4):
            piece = value[16 * group : 16 * group + 16]
            shift = (32 * (group - block)) % LANES
            moved = piece if shift == 0 else pltpu.roll(piece, shift, 1)
            packed = moved if packed is None else jnp.where(lane < 32 * group, packed, moved)
        out_ref[half] = packed


def unpack_window(parts):
    lane = lane_ids(16)
    rows = []
    for group in range(4):
        row = None
        for block in range(4):
            shift = (32 * (block - group)) % LANES
            moved = parts[block] if shift == 0 else pltpu.roll(parts[block], shift, 1)
            row = moved if row is None else jnp.where(lane < 32 * block, row, moved)
        rows.append(row)
    return jnp.concatenate(rows, axis=0)


def point(cf, base, mid, left, right):
    near = cf[base] * mid + cf[base + 1] * pltpu.roll(mid, 1, 0) + cf[base + 2] * pltpu.roll(mid, 63, 0)
    return near + (cf[base + 3] * left + cf[base + 4] * right)


def lanes(u, steps):
    return pltpu.roll(u, steps % LANES, 1)


def stencil(cf, base, u):
    return point(cf, base, u, lanes(u, 1), lanes(u, -1))


def coarse_two(cf, u, r1=None, r2=None):
    left, left2, right, right2 = lanes(u, 1), lanes(u, 2), lanes(u, -1), lanes(u, -2)
    v = point(cf, 5, u, left, right)
    v_left = point(cf, 10, left, left2, u)
    v_right = point(cf, 15, right, u, right2)
    if r1 is not None:
        v, v_left, v_right = v + r1, v_left + lanes(r1, 1), v_right + lanes(r1, -1)
    w = point(cf, 5, v, v_left, v_right)
    if r2 is not None:
        w = w + r2
    return v, w


def coarse_eight(cf, u):
    def body(i, u):
        for _ in range(2):
            u = coarse_two(cf, u)[1]
        return u

    return lax.fori_loop(0, 2, body, u)


def kernel(
    initial, source, rate, velx, vely, strengths, guess, ob,
    amp, gb, fb, ib, sb, sf, sp, rb, rp, pb, cf, rx, rd, pk, pe, lr, ul, lw, e_in, po,
    ld, s1, r1, s0, r0, sq, rq, s2, r2, r4, s3, r3, ready,
):
    t, s = lax.axis_index("tm"), lax.axis_index("space")
    z, x = t // NX_DEV, t % NX_DEV
    c = strip_of(x, s)
    c_lo, c_hi = (c + STRIPS - 1) % STRIPS, (c + 1) % STRIPS
    gives_next = jnp.logical_and(x == NX_DEV - 1, z < NZ - 1)
    gives_first = jnp.logical_and(x == 0, z == 0)
    gives = jnp.logical_or(gives_next, gives_first)

    def at(plane, strip):
        px, ps = place_of(strip)
        return (plane * NX_DEV + px, ps)

    barrier = pltpu.get_barrier_semaphore()

    def greet(device):
        pl.semaphore_signal(barrier, inc=1, device_id=device, device_id_type=pl.DeviceIdType.MESH)

    def mate(dx, dy, dc):
        ps = (s + 2 * dy) % NS
        return (x + dx) % NX_DEV, ps if dc == 0 else ps + 1 - 2 * (s % 2)

    for offset in OFFSETS[:-1]:
        px, ps = mate(*offset)
        greet((z * NX_DEV + px, ps))

    def greet_before(i, _):
        greet(((z - 1) * NX_DEV + NX_DEV - 1, i))
        return 0

    lax.fori_loop(0, jnp.where(z > 0, NS, 0), greet_before, 0)

    def greet_three(plane):
        greet(at(plane, c_lo))
        greet(at(plane, c))
        greet(at(plane, c_hi))

    @pl.when(z == 0)
    def _():
        for plane in range(1, 4):
            greet(at(plane, c))
        for plane in range(4, NZ):
            greet_three(plane)

    def greet_upper(plane, _):
        greet(at(plane, c))
        return 0

    lax.fori_loop(4, jnp.maximum(z, 4), greet_upper, 0)

    @pl.when(z == 7)
    def _():
        greet(at(4, c_lo))
        greet(at(4, c_hi))

    load_guess = pltpu.make_async_copy(guess, gb, ld.at[0])
    load_guess.start()
    load_amp = pltpu.make_async_copy(strengths, amp, ld.at[3])
    load_amp.start()
    load_fields = [
        pltpu.make_async_copy(field, fb.at[which], ld.at[4 + which])
        for which, field in enumerate((rate, velx, vely, source))
    ]
    for load in load_fields:
        load.start()

    @pl.when(gives_first)
    def _():
        pltpu.make_async_copy(initial, ib, ld.at[2]).start()

    @pl.when(gives_next)
    def _():
        pltpu.make_async_copy(guess.at[1], ib, ld.at[2]).start()

    load_guess.wait()
    load_amp.wait()

    lane8 = lane_ids(8)

    def windows(tile_of, put):
        low = [pltpu.roll(tile_of(k), 32, 1) for k in range(16)]
        for k in range(16):
            put(2 * k, jnp.where(lane8 < 32, low[k - 1], low[k]))
        high = [pltpu.roll(tile_of(k), 96, 1) for k in range(16)]
        for k in range(16):
            put(2 * k + 1, jnp.where(lane8 < 96, high[k], high[(k + 1) % 16]))

    for i in range(2):

        def put_guess(strip, value, i=i):
            for m in range(M):
                value = jnp.where(lane8 == m, amp[M * i + m], value)
            sb[strip, i] = value

        windows(lambda k, i=i: gb[i, :, LANES * k : LANES * (k + 1)], put_guess)

    for load in load_fields:
        load.wait()
    for y in range(4):
        k = 4 * y + (x if y % 2 == 0 else 3 - x)
        before, here, after = (
            pl.ds(pl.multiple_of(LANES * ((k + move) % 16), LANES), LANES) for move in (15, 0, 1)
        )
        for f in range(4):
            tile = fb[f, :, here]
            sf[2 * y, f] = jnp.where(
                lane8 < 32, pltpu.roll(fb[f, :, before], 32, 1), pltpu.roll(tile, 32, 1)
            )
            sf[2 * y + 1, f] = jnp.where(
                lane8 < 96, pltpu.roll(tile, 96, 1), pltpu.roll(fb[f, :, after], 96, 1)
            )

    @pl.when(gives)
    def _():
        pltpu.make_async_copy(initial, ib, ld.at[2]).wait()

        def put_before(strip, value):
            sp[strip] = value

        windows(lambda k: ib[:, LANES * k : LANES * (k + 1)], put_before)

    hubs = jnp.where(z == 0, 0, jnp.where(z < 4, 1, 3))
    uppers = jnp.where(z == 4, 5, jnp.where(z == 5, 2, jnp.where(z == 6, 1, 0)))
    pl.semaphore_wait(barrier, STRIPS - 1 + jnp.where(gives_next, STRIPS, 0) + hubs + uppers)

    def signal_ready(strip):
        pl.semaphore_signal(
            ready.at[z], inc=1, device_id=at(0, strip), device_id_type=pl.DeviceIdType.MESH
        )

    @pl.when(z > 0)
    def _():
        signal_ready(c)

    @pl.when(z >= 4)
    def _():
        signal_ready(c_lo)
        signal_ready(c_hi)

    mine = rb.at[pl.ds(2 * x, 2), pl.ds(8 * s, 8)]
    mine_fields = rp.at[:, pl.ds(8 * s, 8)]

    ahead = pb.at[pl.ds(8 * s, 8)]

    @pl.when(gives)
    def _():
        to = jnp.where(gives_next, z + 1, 0)

        def give(offset):
            px, ps = mate(*offset)
            pltpu.make_async_remote_copy(
                sp.at[strip_of(px, ps)], ahead, sq, rq, (to * NX_DEV + px, ps), pl.DeviceIdType.MESH
            ).start()

        for offset in OFFSETS[:-1]:
            give(offset)

        @pl.when(gives_next)
        def _():
            give(OFFSETS[-1])

        @pl.when(gives_first)
        def _():
            pltpu.make_async_copy(sp.at[c], ahead, rq).start()

    for offset in OFFSETS[:-1]:
        px, ps = mate(*offset)
        if offset[0] == 0:
            pltpu.make_async_remote_copy(
                sf.at[ps], mine_fields, s0, r0, (z * NX_DEV + px, ps), pl.DeviceIdType.MESH
            ).start()
    for offset in OFFSETS[:-1]:
        px, ps = mate(*offset)
        pltpu.make_async_remote_copy(
            sb.at[strip_of(px, ps)], mine, s1, r1, (z * NX_DEV + px, ps), pl.DeviceIdType.MESH
        ).start()
    pltpu.make_async_copy(sb.at[c], mine, r1).start()
    pltpu.make_async_copy(sf.at[s], mine_fields, r0).start()
    pltpu.make_async_copy(rp, rp, r0).wait()

    d, a, b = rp[0], rp[1], rp[2]
    row = lax.broadcasted_iota(jnp.int32, (64, LANES), 0)
    col = lax.broadcasted_iota(jnp.int32, (64, LANES), 1) + (64 * c - 32)
    zero = jnp.zeros((64, LANES), jnp.float32)
    c_mid = 1.0 - (4.0 * d + (jnp.abs(a) + jnp.abs(b)))
    c_xm = jnp.where(row == 0, zero, d + jnp.maximum(a, 0.0))
    c_xp = jnp.where(row == 63, zero, d - jnp.minimum(a, 0.0))
    c_ym = jnp.where(col == 0, zero, d + jnp.maximum(b, 0.0))
    c_yp = jnp.where(col == 2047, zero, d - jnp.minimum(b, 0.0))
    cf[0], cf[1], cf[2], cf[3], cf[4] = c_mid, c_xm, c_xp, c_ym, c_yp
    cf[5] = 1.0 - float(M) * (4.0 * d + (jnp.abs(a) + jnp.abs(b)))
    cf[6], cf[7], cf[8], cf[9] = M * c_xm, M * c_xp, M * c_ym, M * c_yp
    for k in range(5):
        cf[10 + k] = lanes(cf[5 + k], 1)
        cf[15 + k] = lanes(cf[5 + k], -1)

    pltpu.make_async_copy(rb, rb, r1).wait()
    pltpu.make_async_copy(pb, pb, rq).wait()

    def forced(u, tile, m):
        strength = jnp.broadcast_to(rb[tile, 0:8, m : m + 1], (8, LANES))
        push = rp[3].reshape(8, 8, LANES) * strength[None]
        return stencil(cf, 0, u) + push.reshape(64, LANES)

    tiles = list(range(8))
    state = [pb[...]] + [rb[tile] for tile in tiles[:-1]]
    for m in range(M):
        state = [forced(u, tile, m) for u, tile in zip(state, tiles)]
    for k in range(8):
        rx[k] = state[k]
    state = [u - rb[tile] for u, tile in zip(state, tiles)]
    for m in range(M):
        state = [stencil(cf, 0, u) for u in state]
    for k in range(8):
        rd[k] = state[k]

    entry = jnp.where(z == 0, rx[0] - rx[0], zero)
    def send_main(packed, plane, slot, sem):
        pltpu.make_async_remote_copy(
            packed, lr.at[slot, pl.ds(1, 2)], s2.at[sem], r2.at[slot], at(plane, c), pl.DeviceIdType.MESH
        ).start()

    def send_sides(packed, plane, slot, sem):
        for src, part, strip in ((packed.at[0], 3, c_lo), (packed.at[1], 0, c_hi)):
            pltpu.make_async_remote_copy(
                src, lr.at[slot, part], s2.at[sem], r2.at[slot], at(plane, strip), pl.DeviceIdType.MESH
            ).start()

    def send_three(packed, plane, slot, sem):
        send_main(packed, plane, slot, sem)
        send_sides(packed, plane, slot, sem)

    def send_window(window, plane, slot, sem):
        pltpu.make_async_remote_copy(
            window, ul.at[slot], s2.at[sem], r4.at[slot], at(plane, c), pl.DeviceIdType.MESH
        ).start()

    def window_arrived(slot):
        pltpu.make_async_copy(ul.at[slot], ul.at[slot], r4.at[slot]).wait()

    def arrived(slot):
        pltpu.make_async_copy(lr.at[slot], lr.at[slot], r2.at[slot]).wait()
        return unpack_window([lr[slot, h] for h in range(4)])

    lane64 = lane_ids(64)

    def chain(err):
        for xx in range(NX_DEV):
            first = rx[2 * xx] + err
            mid, err = coarse_two(cf, err, rd[2 * xx], rd[2 * xx + 1])
            second = rx[2 * xx + 1] + mid
            po[xx] = jnp.where(lane64 < 64, pltpu.roll(first, 96, 1), pltpu.roll(second, 32, 1))
        return err

    def send_results():
        for offset in OFFSETS[:-1]:
            px, ps = mate(*offset)
            pltpu.make_async_remote_copy(
                po.at[px, pl.ds(8 * ps, 8)], ob.at[c], s3, r3, (z * NX_DEV + px, ps), pl.DeviceIdType.MESH
            ).start()
        pltpu.make_async_copy(po.at[x, pl.ds(8 * s, 8)], ob.at[c], r3).start()

    @pl.when(z == 0)
    def _():
        e = chain(entry)
        lw[0] = e
        pack_halves(e, pk)
        send_sides(pk, 0, 0, 0)
        pltpu.make_async_copy(pk, lr.at[0, pl.ds(1, 2)], r2.at[0]).start()
        pl.semaphore_wait(ready.at[1], 1)
        send_window(lw.at[0], 1, 0, 1)
        send_results()
        e = arrived(0)
        for j in range(1, 4):
            e = coarse_eight(cf, e)
            window_arrived(j - 1)
            e = e + ul[j - 1]
            if j < 3:
                lw[j] = e
                pl.semaphore_wait(ready.at[j + 1], 1)
                send_window(lw.at[j], j + 1, 0, j + 1)
        pack_halves(e, pe)
        for plane in (7, 6, 5, 4):
            pl.semaphore_wait(ready.at[plane], 3)
            send_three(pe, plane, 0, plane)

    @pl.when(z > 0)
    def _():
        local_last = zero
        for k in range(0, 8, 2):
            local_last = coarse_two(cf, local_last, rd[k], rd[k + 1])[1]
        lw[0] = local_last

    @pl.when(jnp.logical_and(z >= 1, z <= 3))
    def _():
        send_window(lw.at[0], 0, z - 1, 1)

    @pl.when(z == 4)
    def _():
        pack_halves(lw[0], pk)
        send_three(pk, 7, 1, 7)

    for plane in (7, 6, 5):

        @pl.when(jnp.logical_and(z >= (5 if plane == 7 else 4), z < plane))
        def _(plane=plane):
            send_window(lw.at[0], plane, z - 4, plane)

    for j in range(4, 7):

        @pl.when(jnp.logical_and(z > j, z < 7) if j == 4 else z > j)
        def _(j=j):
            window_arrived(j - 4)

    @pl.when(z == 7)
    def _():
        ul[0] = arrived(1)

    @pl.when(jnp.logical_and(z >= 1, z <= 3))
    def _():
        window_arrived(0)
        e_in[...] = ul[0]

    @pl.when(z >= 4)
    def _():
        e_in[...] = lax.fori_loop(
            0, jnp.maximum(z - 4, 0), lambda j, e: coarse_eight(cf, e) + ul[j], arrived(0)
        )

    @pl.when(z > 0)
    def _():
        chain(e_in[...])
        send_results()

    pltpu.make_async_copy(ob, ob, r3).wait()

    sent = sb.at[pl.ds(0, STRIPS - 1)]
    pltpu.make_async_copy(sent, sent, s1).wait()
    sent_fields = sf.at[pl.ds(0, NS - 1)]
    pltpu.make_async_copy(sent_fields, sent_fields, s0).wait()

    @pl.when(gives_next)
    def _():
        pltpu.make_async_copy(sp, sp, sq).wait()

    @pl.when(gives_first)
    def _():
        most = sp.at[pl.ds(0, STRIPS - 1)]
        pltpu.make_async_copy(most, most, sq).wait()

    @pl.when(z == 0)
    def _():
        pltpu.make_async_copy(pk, pk, s2.at[0]).wait()
        for plane in range(1, NZ):
            pltpu.make_async_copy(lr.at[0], lr.at[0], s2.at[plane]).wait()

    @pl.when(jnp.logical_and(z >= 1, z <= 3))
    def _():
        pltpu.make_async_copy(lr.at[0], lr.at[0], s2.at[1]).wait()

    for plane in (7, 6, 5):

        @pl.when(jnp.logical_and(z >= 4, z < plane))
        def _(plane=plane):
            pltpu.make_async_copy(lr.at[0], lr.at[0], s2.at[plane]).wait()

    gone = ob.at[pl.ds(0, STRIPS - 1)]
    pltpu.make_async_copy(gone, gone, s3).wait()


def place_rows(ob, out):
    lane8 = lane_ids(8)
    for p in range(16):
        left, right = ob[2 * p], ob[2 * p + 1]
        here = slice(LANES * p, LANES * (p + 1))
        out[0, :, here] = jnp.where(lane8 < 64, left, pltpu.roll(right, 64, 1))
        out[1, :, here] = jnp.where(lane8 < 64, pltpu.roll(left, 64, 1), right)


def per_device(*blocks):
    any_space = pl.BlockSpec(memory_space=pl.ANY)
    f32 = functools.partial(pltpu.VMEM, dtype=jnp.float32)
    sem = pltpu.SemaphoreType.DMA
    strips = pl.pallas_call(
        kernel,
        out_shape=jax.ShapeDtypeStruct((STRIPS, 8, LANES), jnp.float32),
        in_specs=[any_space] * 7,
        out_specs=any_space,
        scratch_shapes=[
            pltpu.SMEM((8,), jnp.float32),
            f32((2, 8, 2048)),
            f32((4, 8, 2048)),
            f32((8, 2048)),
            f32((STRIPS, 2, 8, LANES)),
            f32((NS, 4, 8, LANES)),
            f32((STRIPS, 8, LANES)),
            f32((8, 64, LANES)),
            f32((4, 64, LANES)),
            f32((64, LANES)),
            f32((20, 64, LANES)),
            f32((8, 64, LANES)),
            f32((8, 64, LANES)),
            f32((2, 16, LANES)),
            f32((2, 16, LANES)),
            f32((2, 4, 16, LANES)),
            f32((3, 64, LANES)),
            f32((3, 64, LANES)),
            f32((64, LANES)),
            f32((NX_DEV, 64, LANES)),
            sem((8,)),
            sem,
            sem,
            sem,
            sem,
            sem,
            sem,
            sem((8,)),
            sem((2,)),
            sem((3,)),
            sem,
            sem,
            pltpu.SemaphoreType.REGULAR((NZ,)),
        ],
        compiler_params=pltpu.CompilerParams(
            collective_id=0, has_side_effects=True, vmem_limit_bytes=56 * 1024 * 1024
        ),
        cost_estimate=pl.CostEstimate(flops=20_000_000, bytes_accessed=700_000, transcendentals=0),
        name="cycle",
    )(*blocks)
    in_vmem = pl.BlockSpec(memory_space=pltpu.VMEM)
    return pl.pallas_call(
        place_rows,
        out_shape=jax.ShapeDtypeStruct((2, 8, 2048), jnp.float32),
        in_specs=[in_vmem],
        out_specs=in_vmem,
        name="place",
    )(strips)


def solution(mesh):
    in_specs = (
        P("space", None),
        P("space", None),
        P("space", None),
        P("space", None),
        P("space", None),
        P("tm"),
        P("tm", "space", None),
    )
    out_specs = P("tm", "space", None)
    return jax.shard_map(
        per_device, mesh=mesh, in_specs=in_specs, out_specs=out_specs, check_vma=False
    )
```

```python
import functools

import jax
import jax.numpy as jnp
from jax import lax
from jax.experimental import pallas as pl
from jax.experimental.pallas import tpu as pltpu
from jax.sharding import PartitionSpec as P

M = 4
NZ = 8
NX_DEV = 4
NS = 8
STRIPS = 32
LANES = 128


OFFSETS = sorted(
    ((dx, dy, dc) for dx in range(4) for dy in range(4) for dc in range(2)),
    key=lambda o: (-min(o[0], 4 - o[0]) - min(o[1], 4 - o[1]), -o[2]),
)


def div(a, b):
    return lax.div(a, jnp.int32(b))


def rem(a, b):
    return lax.rem(a, jnp.int32(b))


def place_of(strip):
    chip, core = div(strip, 2), rem(strip, 2)
    y, q = div(chip, 4), rem(chip, 4)
    x = q + rem(y, 2) * (3 - 2 * q)
    return x, 2 * y + core


def strip_of(x, s):
    y, core = div(s, 2), rem(s, 2)
    q = x + rem(y, 2) * (3 - 2 * x)
    return 2 * (4 * y + q) + core


def lane_ids(rows):
    return lax.broadcasted_iota(jnp.int32, (rows, LANES), 1)


def pack_halves(value, out_ref):
    lane = lane_ids(16)
    for half in range(2):
        block = 1 + half
        packed = None
        for group in range(4):
            piece = value[16 * group : 16 * group + 16]
            shift = (32 * (group - block)) % LANES
            moved = piece if shift == 0 else pltpu.roll(piece, shift, 1)
            packed = moved if packed is None else jnp.where(lane < 32 * group, packed, moved)
        out_ref[half] = packed


def unpack_window(parts):
    lane = lane_ids(16)
    rows = []
    for group in range(4):
        row = None
        for block in range(4):
            shift = (32 * (block - group)) % LANES
            moved = parts[block] if shift == 0 else pltpu.roll(parts[block], shift, 1)
            row = moved if row is None else jnp.where(lane < 32 * block, row, moved)
        rows.append(row)
    return jnp.concatenate(rows, axis=0)


def point(cf, base, mid, left, right):
    near = cf[base] * mid + cf[base + 1] * pltpu.roll(mid, 1, 0) + cf[base + 2] * pltpu.roll(mid, 63, 0)
    return near + (cf[base + 3] * left + cf[base + 4] * right)


def lanes(u, steps):
    return pltpu.roll(u, steps % LANES, 1)


def stencil(cf, base, u):
    return point(cf, base, u, lanes(u, 1), lanes(u, -1))


def coarse_two(cf, u, r1=None, r2=None):
    left, left2, right, right2 = lanes(u, 1), lanes(u, 2), lanes(u, -1), lanes(u, -2)
    v = point(cf, 5, u, left, right)
    v_left = point(cf, 10, left, left2, u)
    v_right = point(cf, 15, right, u, right2)
    if r1 is not None:
        v, v_left, v_right = v + r1, v_left + lanes(r1, 1), v_right + lanes(r1, -1)
    w = point(cf, 5, v, v_left, v_right)
    if r2 is not None:
        w = w + r2
    return v, w


def coarse_eight(cf, u):
    def body(i, u):
        for _ in range(2):
            u = coarse_two(cf, u)[1]
        return u

    return lax.fori_loop(0, 2, body, u)


def kernel(
    initial, source, rate, velx, vely, strengths, guess, ob,
    amp, gb, fb, ib, sb, sf, sp, rb, rp, pb, cf, rx, rd, pk, pe, lr, ul, lw, e_in, ahead_3, po,
    ld, s1, r1, s0, r0, sq, rq, s2, r2, r4, s3, r3, ready,
):
    t, s = lax.axis_index("tm"), lax.axis_index("space")
    z, x = div(t, NX_DEV), rem(t, NX_DEV)
    c = strip_of(x, s)
    lo, here, hi = place_of(rem(c + STRIPS - 1, STRIPS)), (x, s), place_of(rem(c + 1, STRIPS))
    xs = [rem(x + dx, NX_DEV) for dx in range(NX_DEV)]
    other = 1 - 2 * rem(s, 2)
    ss = [rem(s + 2 * dy, NS) for dy in range(4)]
    mates = {(dx, dy, dc): (xs[dx], ss[dy] + other * dc) for dx, dy, dc in OFFSETS}

    gives_next = jnp.logical_and(x == NX_DEV - 1, z < NZ - 1)
    gives_first = jnp.logical_and(x == 0, z == 0)
    gives = jnp.logical_or(gives_next, gives_first)

    def at(plane, place):
        return (plane * NX_DEV + place[0], place[1])

    barrier = pltpu.get_barrier_semaphore()

    def greet(device):
        pl.semaphore_signal(barrier, inc=1, device_id=device, device_id_type=pl.DeviceIdType.MESH)

    for offset in OFFSETS[:-1]:
        px, ps = mates[offset]
        greet((z * NX_DEV + px, ps))

    def greet_before(i, _):
        greet(((z - 1) * NX_DEV + NX_DEV - 1, i))
        return 0

    lax.fori_loop(0, jnp.where(z > 0, NS, 0), greet_before, 0)

    def greet_three(plane):
        greet(at(plane, lo))
        greet(at(plane, here))
        greet(at(plane, hi))

    @pl.when(z == 0)
    def _():
        for plane in range(1, 4):
            greet(at(plane, here))
        for plane in range(4, NZ):
            greet_three(plane)

    def greet_upper(plane, _):
        greet(at(plane, here))
        return 0

    first_upper = jnp.where(z == 7, 4, 3)
    lax.fori_loop(first_upper, jnp.maximum(z, first_upper), greet_upper, 0)

    @pl.when(z >= 6)
    def _():
        greet(at(z - 3, lo))
        greet(at(z - 3, hi))

    @pl.when(z == 7)
    def _():
        greet_three(3)

    load_guess = pltpu.make_async_copy(guess, gb, ld.at[0])
    load_guess.start()
    load_amp = pltpu.make_async_copy(strengths, amp, ld.at[3])
    load_amp.start()
    load_fields = [
        pltpu.make_async_copy(field, fb.at[which], ld.at[4 + which])
        for which, field in enumerate((rate, velx, vely, source))
    ]
    for load in load_fields:
        load.start()

    @pl.when(gives_first)
    def _():
        pltpu.make_async_copy(initial, ib, ld.at[2]).start()

    @pl.when(gives_next)
    def _():
        pltpu.make_async_copy(guess.at[1], ib, ld.at[2]).start()

    load_guess.wait()
    load_amp.wait()

    lane8 = lane_ids(8)

    def windows(tile_of, put):
        low = [pltpu.roll(tile_of(k), 32, 1) for k in range(16)]
        for k in range(16):
            put(2 * k, jnp.where(lane8 < 32, low[k - 1], low[k]))
        high = [pltpu.roll(tile_of(k), 96, 1) for k in range(16)]
        for k in range(16):
            put(2 * k + 1, jnp.where(lane8 < 96, high[k], high[(k + 1) % 16]))

    for i in range(2):

        def put_guess(strip, value, i=i):
            for m in range(M):
                value = jnp.where(lane8 == m, amp[M * i + m], value)
            sb[strip, i] = value

        windows(lambda k, i=i: gb[i, :, LANES * k : LANES * (k + 1)], put_guess)

    for load in load_fields:
        load.wait()
    for y in range(4):
        k = 4 * y + (x if y % 2 == 0 else 3 - x)
        k_lo, k_at, k_hi = (
            pl.ds(pl.multiple_of(LANES * ((k + move) % 16), LANES), LANES) for move in (15, 0, 1)
        )
        for f in range(4):
            tile = fb[f, :, k_at]
            sf[2 * y, f] = jnp.where(
                lane8 < 32, pltpu.roll(fb[f, :, k_lo], 32, 1), pltpu.roll(tile, 32, 1)
            )
            sf[2 * y + 1, f] = jnp.where(
                lane8 < 96, pltpu.roll(tile, 96, 1), pltpu.roll(fb[f, :, k_hi], 96, 1)
            )

    @pl.when(gives)
    def _():
        pltpu.make_async_copy(initial, ib, ld.at[2]).wait()

        def put_before(strip, value):
            sp[strip] = value

        windows(lambda k: ib[:, LANES * k : LANES * (k + 1)], put_before)

    hubs = jnp.where(z == 0, 0, jnp.where(z < 4, 1, 3))
    uppers = jnp.where(z == 3, 8, jnp.where(z == 4, 5, jnp.where(z == 5, 2, jnp.where(z == 6, 1, 0))))
    pl.semaphore_wait(barrier, STRIPS - 1 + jnp.where(gives_next, STRIPS, 0) + hubs + uppers)

    def signal_ready(place):
        pl.semaphore_signal(
            ready.at[z], inc=1, device_id=at(0, place), device_id_type=pl.DeviceIdType.MESH
        )

    @pl.when(z > 0)
    def _():
        signal_ready(here)

    @pl.when(z >= 4)
    def _():
        signal_ready(lo)
        signal_ready(hi)

    mine = rb.at[pl.ds(2 * x, 2), pl.ds(8 * s, 8)]
    mine_fields = rp.at[:, pl.ds(8 * s, 8)]

    ahead = pb.at[pl.ds(8 * s, 8)]

    @pl.when(gives)
    def _():
        to = jnp.where(gives_next, z + 1, 0)

        def give(offset):
            px, ps = mates[offset]
            pltpu.make_async_remote_copy(
                sp.at[strip_of(px, ps)], ahead, sq, rq, (to * NX_DEV + px, ps), pl.DeviceIdType.MESH
            ).start()

        for offset in OFFSETS[:-1]:
            give(offset)

        @pl.when(gives_next)
        def _():
            give(OFFSETS[-1])

        @pl.when(gives_first)
        def _():
            pltpu.make_async_copy(sp.at[c], ahead, rq).start()

    for offset in OFFSETS[:-1]:
        px, ps = mates[offset]
        if offset[0] == 0:
            pltpu.make_async_remote_copy(
                sf.at[ps], mine_fields, s0, r0, (z * NX_DEV + px, ps), pl.DeviceIdType.MESH
            ).start()
    for offset in OFFSETS[:-1]:
        px, ps = mates[offset]
        pltpu.make_async_remote_copy(
            sb.at[strip_of(px, ps)], mine, s1, r1, (z * NX_DEV + px, ps), pl.DeviceIdType.MESH
        ).start()
    pltpu.make_async_copy(sb.at[c], mine, r1).start()
    pltpu.make_async_copy(sf.at[s], mine_fields, r0).start()
    pltpu.make_async_copy(rp, rp, r0).wait()

    d, a, b = rp[0], rp[1], rp[2]
    row = lax.broadcasted_iota(jnp.int32, (64, LANES), 0)
    col = lax.broadcasted_iota(jnp.int32, (64, LANES), 1) + (64 * c - 32)
    zero = jnp.zeros((64, LANES), jnp.float32)
    c_mid = 1.0 - (4.0 * d + (jnp.abs(a) + jnp.abs(b)))
    c_xm = jnp.where(row == 0, zero, d + jnp.maximum(a, 0.0))
    c_xp = jnp.where(row == 63, zero, d - jnp.minimum(a, 0.0))
    c_ym = jnp.where(col == 0, zero, d + jnp.maximum(b, 0.0))
    c_yp = jnp.where(col == 2047, zero, d - jnp.minimum(b, 0.0))
    cf[0], cf[1], cf[2], cf[3], cf[4] = c_mid, c_xm, c_xp, c_ym, c_yp
    cf[5] = 1.0 - float(M) * (4.0 * d + (jnp.abs(a) + jnp.abs(b)))
    cf[6], cf[7], cf[8], cf[9] = M * c_xm, M * c_xp, M * c_ym, M * c_yp
    for k in range(5):
        cf[10 + k] = lanes(cf[5 + k], 1)
        cf[15 + k] = lanes(cf[5 + k], -1)

    pltpu.make_async_copy(rb, rb, r1).wait()
    pltpu.make_async_copy(pb, pb, rq).wait()

    def forced(u, tile, m):
        strength = jnp.broadcast_to(rb[tile, 0:8, m : m + 1], (8, LANES))
        push = rp[3].reshape(8, 8, LANES) * strength[None]
        return stencil(cf, 0, u) + push.reshape(64, LANES)

    tiles = list(range(8))
    state = [pb[...]] + [rb[tile] for tile in tiles[:-1]]
    for m in range(M):
        state = [forced(u, tile, m) for u, tile in zip(state, tiles)]
    for k in range(8):
        rx[k] = state[k]
    state = [u - rb[tile] for u, tile in zip(state, tiles)]
    for m in range(M):
        state = [stencil(cf, 0, u) for u in state]
    for k in range(8):
        rd[k] = state[k]

    entry = jnp.where(z == 0, rx[0] - rx[0], zero)
    def send_main(packed, plane, slot, sem):
        pltpu.make_async_remote_copy(
            packed, lr.at[slot, pl.ds(1, 2)], s2.at[sem], r2.at[slot], at(plane, here), pl.DeviceIdType.MESH
        ).start()

    def send_sides(packed, plane, slot, sem):
        for src, part, side in ((packed.at[0], 3, lo), (packed.at[1], 0, hi)):
            pltpu.make_async_remote_copy(
                src, lr.at[slot, part], s2.at[sem], r2.at[slot], at(plane, side), pl.DeviceIdType.MESH
            ).start()

    def send_three(packed, plane, slot, sem):
        send_main(packed, plane, slot, sem)
        send_sides(packed, plane, slot, sem)

    def send_window(window, plane, slot, sem):
        pltpu.make_async_remote_copy(
            window, ul.at[slot], s2.at[sem], r4.at[slot], at(plane, here), pl.DeviceIdType.MESH
        ).start()

    def window_arrived(slot):
        pltpu.make_async_copy(ul.at[slot], ul.at[slot], r4.at[slot]).wait()

    def arrived(slot):
        pltpu.make_async_copy(lr.at[slot], lr.at[slot], r2.at[slot]).wait()
        return unpack_window([lr[slot, h] for h in range(4)])

    lane64 = lane_ids(64)

    def send_results(xx):
        for offset in OFFSETS:
            if offset[0] == 0 and offset != OFFSETS[-1]:
                ps = mates[offset][1]
                pltpu.make_async_remote_copy(
                    po.at[xx, pl.ds(8 * ps, 8)], ob.at[c], s3, r3, (z * NX_DEV + xx, ps), pl.DeviceIdType.MESH
                ).start()
        mine_out = po.at[xx, pl.ds(8 * s, 8)]

        @pl.when(x == xx)
        def _():
            pltpu.make_async_copy(mine_out, ob.at[c], r3).start()

        @pl.when(x != xx)
        def _():
            pltpu.make_async_remote_copy(
                mine_out, ob.at[c], s3, r3, (z * NX_DEV + xx, s), pl.DeviceIdType.MESH
            ).start()

    def chain(err, ready_made):
        for xx in range(NX_DEV):
            first = rx[2 * xx] + err
            mid, err = coarse_two(cf, err, rd[2 * xx], rd[2 * xx + 1])
            second = rx[2 * xx + 1] + mid
            po[xx] = jnp.where(lane64 < 64, pltpu.roll(first, 96, 1), pltpu.roll(second, 32, 1))
            ready_made(xx)
        return err

    @pl.when(z == 0)
    def _():
        def pass_on(e, which, planes):
            pack_halves(e, pe.at[which])
            for plane in planes:
                pl.semaphore_wait(ready.at[plane], 3)
                send_three(pe.at[which], plane, 0, plane)

        e = chain(entry, lambda xx: None)
        lw[0] = e
        pack_halves(e, pk)
        send_sides(pk, 0, 0, 0)
        pltpu.make_async_copy(pk, lr.at[0, pl.ds(1, 2)], r2.at[0]).start()
        pl.semaphore_wait(ready.at[1], 1)
        send_window(lw.at[0], 1, 0, 1)
        for xx in range(NX_DEV):
            send_results(xx)
        e = arrived(0)
        for j in range(1, 3):
            e = coarse_eight(cf, e)
            window_arrived(j - 1)
            e = e + ul[j - 1]
            lw[j] = e
            pl.semaphore_wait(ready.at[j + 1], 1)
            send_window(lw.at[j], j + 1, 0, j + 1)
        pass_on(e, 0, (6, 5, 4))
        pass_on(coarse_eight(cf, e), 1, (7,))

    @pl.when(z > 0)
    def _():
        local_last = zero
        for k in range(0, 8, 2):
            local_last = coarse_two(cf, local_last, rd[k], rd[k + 1])[1]
        lw[0] = local_last

    @pl.when(jnp.logical_and(z >= 1, z <= 2))
    def _():
        send_window(lw.at[0], 0, z - 1, 1)

    @pl.when(jnp.logical_or(z == 3, z == 4))
    def _():
        pack_halves(lw[0], pk)

    @pl.when(z == 3)
    def _():
        send_three(pk, 7, 2, 7)

    for plane in (7, 6, 5, 4):
        if plane >= 6:

            @pl.when(z == plane - 3)
            def _(plane=plane):
                send_three(pk, plane, 1, plane)

        @pl.when(jnp.logical_and(z >= (3 if plane < 6 else plane - 2), z < plane))
        def _(plane=plane):
            send_window(lw.at[0], plane, z - (4 if plane == 7 else 3), plane)

    for slot in range(3):

        @pl.when((z == 4) | (z == 5) if slot == 0 else z >= 4 + slot)
        def _(slot=slot):
            window_arrived(slot)

    @pl.when(z >= 6)
    def _():
        ul[0] = arrived(1)

    ahead_3[...] = zero

    @pl.when(z == 7)
    def _():
        ahead_3[...] = arrived(2)

    @pl.when(jnp.logical_and(z >= 1, z <= 3))
    def _():
        window_arrived(0)
        e_in[...] = ul[0]

    @pl.when(z >= 4)
    def _():
        e_in[...] = lax.fori_loop(
            0, jnp.minimum(z - 3, 3), lambda j, e: coarse_eight(cf, e) + ul[j], arrived(0) + ahead_3[...]
        )

    @pl.when(z > 0)
    def _():
        chain(e_in[...], send_results)

    pltpu.make_async_copy(ob, ob, r3).wait()

    sent = sb.at[pl.ds(0, STRIPS - 1)]
    pltpu.make_async_copy(sent, sent, s1).wait()
    sent_fields = sf.at[pl.ds(0, NS - 1)]
    pltpu.make_async_copy(sent_fields, sent_fields, s0).wait()

    @pl.when(gives_next)
    def _():
        pltpu.make_async_copy(sp, sp, sq).wait()

    @pl.when(gives_first)
    def _():
        most = sp.at[pl.ds(0, STRIPS - 1)]
        pltpu.make_async_copy(most, most, sq).wait()

    @pl.when(z == 0)
    def _():
        pltpu.make_async_copy(pk, pk, s2.at[0]).wait()
        for plane in range(1, NZ):
            pltpu.make_async_copy(lr.at[0], lr.at[0], s2.at[plane]).wait()

    @pl.when(jnp.logical_and(z >= 1, z <= 2))
    def _():
        pltpu.make_async_copy(lr.at[0], lr.at[0], s2.at[1]).wait()

    for plane in (7, 6, 5, 4):

        @pl.when(jnp.logical_and(z >= 3, z < plane))
        def _(plane=plane):
            pltpu.make_async_copy(lr.at[0], lr.at[0], s2.at[plane]).wait()

    gone = ob.at[pl.ds(0, STRIPS - 1)]
    pltpu.make_async_copy(gone, gone, s3).wait()


def place_rows(ob, out):
    lane8 = lane_ids(8)
    for p in range(16):
        left, right = ob[2 * p], ob[2 * p + 1]
        here = slice(LANES * p, LANES * (p + 1))
        out[0, :, here] = jnp.where(lane8 < 64, left, pltpu.roll(right, 64, 1))
        out[1, :, here] = jnp.where(lane8 < 64, pltpu.roll(left, 64, 1), right)


def per_device(*blocks):
    any_space = pl.BlockSpec(memory_space=pl.ANY)
    f32 = functools.partial(pltpu.VMEM, dtype=jnp.float32)
    sem = pltpu.SemaphoreType.DMA
    strips = pl.pallas_call(
        kernel,
        out_shape=jax.ShapeDtypeStruct((STRIPS, 8, LANES), jnp.float32),
        in_specs=[any_space] * 7,
        out_specs=any_space,
        scratch_shapes=[
            pltpu.SMEM((8,), jnp.float32),
            f32((2, 8, 2048)),
            f32((4, 8, 2048)),
            f32((8, 2048)),
            f32((STRIPS, 2, 8, LANES)),
            f32((NS, 4, 8, LANES)),
            f32((STRIPS, 8, LANES)),
            f32((8, 64, LANES)),
            f32((4, 64, LANES)),
            f32((64, LANES)),
            f32((20, 64, LANES)),
            f32((8, 64, LANES)),
            f32((8, 64, LANES)),
            f32((2, 16, LANES)),
            f32((2, 2, 16, LANES)),
            f32((3, 4, 16, LANES)),
            f32((3, 64, LANES)),
            f32((3, 64, LANES)),
            f32((64, LANES)),
            f32((64, LANES)),
            f32((NX_DEV, 64, LANES)),
            sem((8,)),
            sem,
            sem,
            sem,
            sem,
            sem,
            sem,
            sem((8,)),
            sem((3,)),
            sem((3,)),
            sem,
            sem,
            pltpu.SemaphoreType.REGULAR((NZ,)),
        ],
        compiler_params=pltpu.CompilerParams(
            collective_id=0, has_side_effects=True, vmem_limit_bytes=56 * 1024 * 1024
        ),
        cost_estimate=pl.CostEstimate(flops=20_000_000, bytes_accessed=700_000, transcendentals=0),
        name="cycle",
    )(*blocks)
    in_vmem = pl.BlockSpec(memory_space=pltpu.VMEM)
    return pl.pallas_call(
        place_rows,
        out_shape=jax.ShapeDtypeStruct((2, 8, 2048), jnp.float32),
        in_specs=[in_vmem],
        out_specs=in_vmem,
        name="place",
    )(strips)


def solution(mesh):
    in_specs = (
        P("space", None),
        P("space", None),
        P("space", None),
        P("space", None),
        P("space", None),
        P("tm"),
        P("tm", "space", None),
    )
    out_specs = P("tm", "space", None)
    return jax.shard_map(
        per_device, mesh=mesh, in_specs=in_specs, out_specs=out_specs, check_vma=False
    )
```

```python
import functools

import jax
import jax.numpy as jnp
from jax import lax
from jax.experimental import pallas as pl
from jax.experimental.pallas import tpu as pltpu
from jax.sharding import PartitionSpec as P

M = 4
NZ = 8
NX_DEV = 4
NS = 8
STRIPS = 32
LANES = 128


OFFSETS = sorted(
    ((dx, dy, dc) for dx in range(4) for dy in range(4) for dc in range(2)),
    key=lambda o: (-min(o[0], 4 - o[0]) - min(o[1], 4 - o[1]), -o[2]),
)


def div(a, b):
    return lax.div(a, jnp.int32(b))


def rem(a, b):
    return lax.rem(a, jnp.int32(b))


def place_of(strip):
    chip, core = div(strip, 2), rem(strip, 2)
    y, q = div(chip, 4), rem(chip, 4)
    x = q + rem(y, 2) * (3 - 2 * q)
    return x, 2 * y + core


def strip_of(x, s):
    y, core = div(s, 2), rem(s, 2)
    q = x + rem(y, 2) * (3 - 2 * x)
    return 2 * (4 * y + q) + core


def lane_ids(rows):
    return lax.broadcasted_iota(jnp.int32, (rows, LANES), 1)


def pack_halves(value, out_ref):
    lane = lane_ids(16)
    for half in range(2):
        block = 1 + half
        packed = None
        for group in range(4):
            piece = value[16 * group : 16 * group + 16]
            shift = (32 * (group - block)) % LANES
            moved = piece if shift == 0 else pltpu.roll(piece, shift, 1)
            packed = moved if packed is None else jnp.where(lane < 32 * group, packed, moved)
        out_ref[half] = packed


def unpack_window(parts):
    lane = lane_ids(16)
    rows = []
    for group in range(4):
        row = None
        for block in range(4):
            shift = (32 * (block - group)) % LANES
            moved = parts[block] if shift == 0 else pltpu.roll(parts[block], shift, 1)
            row = moved if row is None else jnp.where(lane < 32 * block, row, moved)
        rows.append(row)
    return jnp.concatenate(rows, axis=0)


def point(cf, base, mid, left, right):
    near = cf[base] * mid + cf[base + 1] * pltpu.roll(mid, 1, 0) + cf[base + 2] * pltpu.roll(mid, 63, 0)
    return near + (cf[base + 3] * left + cf[base + 4] * right)


def lanes(u, steps):
    return pltpu.roll(u, steps % LANES, 1)


def stencil(cf, base, u):
    return point(cf, base, u, lanes(u, 1), lanes(u, -1))


def coarse_two(cf, u, r1=None, r2=None):
    left, left2, right, right2 = lanes(u, 1), lanes(u, 2), lanes(u, -1), lanes(u, -2)
    v = point(cf, 5, u, left, right)
    v_left = point(cf, 10, left, left2, u)
    v_right = point(cf, 15, right, u, right2)
    if r1 is not None:
        v, v_left, v_right = v + r1, v_left + lanes(r1, 1), v_right + lanes(r1, -1)
    w = point(cf, 5, v, v_left, v_right)
    if r2 is not None:
        w = w + r2
    return v, w


def square_coarse(cf, kf):
    mid, up, down, left, right = (cf[5 + k] for k in range(5))
    at_left, at_right = [cf[10 + k] for k in range(5)], [cf[15 + k] for k in range(5)]
    at_up = [pltpu.roll(cf[5 + k], 1, 0) for k in range(5)]
    at_down = [pltpu.roll(cf[5 + k], 63, 0) for k in range(5)]
    kf[0] = (mid * mid + up * at_up[2] + down * at_down[1]) + (left * at_left[4] + right * at_right[3])
    kf[1] = left * (mid + at_left[0])
    kf[2] = right * (mid + at_right[0])
    kf[3] = left * at_left[3]
    kf[4] = right * at_right[4]
    kf[5] = pltpu.roll(up * at_up[1], 62, 0)
    kf[6] = pltpu.roll(down * at_down[2], 2, 0)
    kf[7] = pltpu.roll(up * (mid + at_up[0]), 63, 0)
    kf[8] = pltpu.roll(up * at_up[3] + left * at_left[1], 63, 0)
    kf[9] = pltpu.roll(up * at_up[4] + right * at_right[1], 63, 0)
    kf[10] = pltpu.roll(down * (mid + at_down[0]), 1, 0)
    kf[11] = pltpu.roll(down * at_down[3] + left * at_left[2], 1, 0)
    kf[12] = pltpu.roll(down * at_down[4] + right * at_right[2], 1, 0)


def coarse_square(kf, u):
    left, left2, right, right2 = lanes(u, 1), lanes(u, 2), lanes(u, -1), lanes(u, -2)
    above = kf[7] * u + (kf[8] * left + kf[9] * right)
    below = kf[10] * u + (kf[11] * left + kf[12] * right)
    far = pltpu.roll(kf[5] * u, 2, 0) + pltpu.roll(kf[6] * u, 62, 0)
    row = (kf[1] * left + kf[2] * right) + (kf[3] * left2 + kf[4] * right2)
    return (kf[0] * u + far + row) + (pltpu.roll(above, 1, 0) + pltpu.roll(below, 63, 0))


def coarse_eight(kf, u):
    for _ in range(4):
        u = coarse_square(kf, u)
    return u


def kernel(
    initial, source, rate, velx, vely, strengths, guess, ob,
    amp, gb, fb, ib, sb, sf, sp, rb, rp, pb, cf, kf, rx, rd, pk, pe, lr, ul, lw, e_in, ahead_3, po,
    ld, s1, r1, s0, r0, sq, rq, s2, r2, r4, s3, r3, ready,
):
    t, s = lax.axis_index("tm"), lax.axis_index("space")
    z, x = div(t, NX_DEV), rem(t, NX_DEV)
    c = strip_of(x, s)
    lo, here, hi = place_of(rem(c + STRIPS - 1, STRIPS)), (x, s), place_of(rem(c + 1, STRIPS))
    xs = [rem(x + dx, NX_DEV) for dx in range(NX_DEV)]
    other = 1 - 2 * rem(s, 2)
    ss = [rem(s + 2 * dy, NS) for dy in range(4)]
    mates = {(dx, dy, dc): (xs[dx], ss[dy] + other * dc) for dx, dy, dc in OFFSETS}

    gives_next = jnp.logical_and(x == NX_DEV - 1, z < NZ - 1)
    gives_first = jnp.logical_and(x == 0, z == 0)
    gives = jnp.logical_or(gives_next, gives_first)

    def at(plane, place):
        return (plane * NX_DEV + place[0], place[1])

    barrier = pltpu.get_barrier_semaphore()

    def greet(device):
        pl.semaphore_signal(barrier, inc=1, device_id=device, device_id_type=pl.DeviceIdType.MESH)

    for offset in OFFSETS[:-1]:
        px, ps = mates[offset]
        greet((z * NX_DEV + px, ps))

    def greet_before(i, _):
        greet(((z - 1) * NX_DEV + NX_DEV - 1, i))
        return 0

    lax.fori_loop(0, jnp.where(z > 0, NS, 0), greet_before, 0)

    def greet_three(plane):
        greet(at(plane, lo))
        greet(at(plane, here))
        greet(at(plane, hi))

    @pl.when(z == 0)
    def _():
        for plane in range(1, 4):
            greet(at(plane, here))
        for plane in range(4, NZ):
            greet_three(plane)

    def greet_upper(plane, _):
        greet(at(plane, here))
        return 0

    lax.fori_loop(4, jnp.maximum(z, 4), greet_upper, 0)

    @pl.when(z == 7)
    def _():
        greet(at(4, lo))
        greet(at(4, hi))

    @pl.when(z == 3)
    def _():
        greet(at(4, here))
        greet(at(5, here))
        greet_three(6)
        greet_three(7)

    load_guess = pltpu.make_async_copy(guess, gb, ld.at[0])
    load_guess.start()
    load_amp = pltpu.make_async_copy(strengths, amp, ld.at[3])
    load_amp.start()
    load_fields = [
        pltpu.make_async_copy(field, fb.at[which], ld.at[4 + which])
        for which, field in enumerate((rate, velx, vely, source))
    ]
    for load in load_fields:
        load.start()

    @pl.when(gives_first)
    def _():
        pltpu.make_async_copy(initial, ib, ld.at[2]).start()

    @pl.when(gives_next)
    def _():
        pltpu.make_async_copy(guess.at[1], ib, ld.at[2]).start()

    load_guess.wait()
    load_amp.wait()

    lane8 = lane_ids(8)

    def windows(tile_of, put):
        low = [pltpu.roll(tile_of(k), 32, 1) for k in range(16)]
        for k in range(16):
            put(2 * k, jnp.where(lane8 < 32, low[k - 1], low[k]))
        high = [pltpu.roll(tile_of(k), 96, 1) for k in range(16)]
        for k in range(16):
            put(2 * k + 1, jnp.where(lane8 < 96, high[k], high[(k + 1) % 16]))

    for i in range(2):

        def put_guess(strip, value, i=i):
            for m in range(M):
                value = jnp.where(lane8 == m, amp[M * i + m], value)
            sb[strip, i] = value

        windows(lambda k, i=i: gb[i, :, LANES * k : LANES * (k + 1)], put_guess)

    for load in load_fields:
        load.wait()
    for y in range(4):
        k = 4 * y + (x if y % 2 == 0 else 3 - x)
        k_lo, k_at, k_hi = (
            pl.ds(pl.multiple_of(LANES * ((k + move) % 16), LANES), LANES) for move in (15, 0, 1)
        )
        for f in range(4):
            tile = fb[f, :, k_at]
            sf[2 * y, f] = jnp.where(
                lane8 < 32, pltpu.roll(fb[f, :, k_lo], 32, 1), pltpu.roll(tile, 32, 1)
            )
            sf[2 * y + 1, f] = jnp.where(
                lane8 < 96, pltpu.roll(tile, 96, 1), pltpu.roll(fb[f, :, k_hi], 96, 1)
            )

    @pl.when(gives)
    def _():
        pltpu.make_async_copy(initial, ib, ld.at[2]).wait()

        def put_before(strip, value):
            sp[strip] = value

        windows(lambda k: ib[:, LANES * k : LANES * (k + 1)], put_before)

    hubs = jnp.where(z == 0, 0, jnp.where(z < 4, 1, 3))
    uppers = jnp.where(z == 4, 5, jnp.where(z == 5, 2, jnp.where(z == 6, 1, 0)))
    from_3 = jnp.where(z >= 6, 3, jnp.where(z >= 4, 1, 0))
    pl.semaphore_wait(barrier, STRIPS - 1 + jnp.where(gives_next, STRIPS, 0) + hubs + uppers + from_3)

    def signal_ready(place, plane=0):
        pl.semaphore_signal(
            ready.at[z], inc=1, device_id=at(plane, place), device_id_type=pl.DeviceIdType.MESH
        )

    @pl.when(z > 0)
    def _():
        signal_ready(here)

    @pl.when(z >= 4)
    def _():
        signal_ready(lo)
        signal_ready(hi)
        signal_ready(here, 3)

    @pl.when(z >= 6)
    def _():
        signal_ready(lo, 3)
        signal_ready(hi, 3)

    mine = rb.at[pl.ds(2 * x, 2), pl.ds(8 * s, 8)]
    mine_fields = rp.at[:, pl.ds(8 * s, 8)]

    ahead = pb.at[pl.ds(8 * s, 8)]

    @pl.when(gives)
    def _():
        to = jnp.where(gives_next, z + 1, 0)

        def give(offset):
            px, ps = mates[offset]
            pltpu.make_async_remote_copy(
                sp.at[strip_of(px, ps)], ahead, sq, rq, (to * NX_DEV + px, ps), pl.DeviceIdType.MESH
            ).start()

        for offset in OFFSETS[:-1]:
            give(offset)

        @pl.when(gives_next)
        def _():
            give(OFFSETS[-1])

        @pl.when(gives_first)
        def _():
            pltpu.make_async_copy(sp.at[c], ahead, rq).start()

    for offset in OFFSETS[:-1]:
        px, ps = mates[offset]
        if offset[0] == 0:
            pltpu.make_async_remote_copy(
                sf.at[ps], mine_fields, s0, r0, (z * NX_DEV + px, ps), pl.DeviceIdType.MESH
            ).start()
    for offset in OFFSETS[:-1]:
        px, ps = mates[offset]
        pltpu.make_async_remote_copy(
            sb.at[strip_of(px, ps)], mine, s1, r1, (z * NX_DEV + px, ps), pl.DeviceIdType.MESH
        ).start()
    pltpu.make_async_copy(sb.at[c], mine, r1).start()
    pltpu.make_async_copy(sf.at[s], mine_fields, r0).start()
    pltpu.make_async_copy(rp, rp, r0).wait()

    d, a, b = rp[0], rp[1], rp[2]
    row = lax.broadcasted_iota(jnp.int32, (64, LANES), 0)
    col = lax.broadcasted_iota(jnp.int32, (64, LANES), 1) + (64 * c - 32)
    zero = jnp.zeros((64, LANES), jnp.float32)
    c_mid = 1.0 - (4.0 * d + (jnp.abs(a) + jnp.abs(b)))
    c_xm = jnp.where(row == 0, zero, d + jnp.maximum(a, 0.0))
    c_xp = jnp.where(row == 63, zero, d - jnp.minimum(a, 0.0))
    c_ym = jnp.where(col == 0, zero, d + jnp.maximum(b, 0.0))
    c_yp = jnp.where(col == 2047, zero, d - jnp.minimum(b, 0.0))
    cf[0], cf[1], cf[2], cf[3], cf[4] = c_mid, c_xm, c_xp, c_ym, c_yp
    cf[5] = 1.0 - float(M) * (4.0 * d + (jnp.abs(a) + jnp.abs(b)))
    cf[6], cf[7], cf[8], cf[9] = M * c_xm, M * c_xp, M * c_ym, M * c_yp
    for k in range(5):
        cf[10 + k] = lanes(cf[5 + k], 1)
        cf[15 + k] = lanes(cf[5 + k], -1)

    pltpu.make_async_copy(rb, rb, r1).wait()
    pltpu.make_async_copy(pb, pb, rq).wait()

    def forced(u, tile, m):
        strength = jnp.broadcast_to(rb[tile, 0:8, m : m + 1], (8, LANES))
        push = rp[3].reshape(8, 8, LANES) * strength[None]
        return stencil(cf, 0, u) + push.reshape(64, LANES)

    def fine(intervals):
        state = [pb[...] if k == 0 else rb[k - 1] for k in intervals]
        for m in range(M):
            state = [forced(u, k, m) for u, k in zip(state, intervals)]
        relaxed = state
        for u, k in zip(relaxed, intervals):
            rx[k] = u
        state = [u - rb[k] for u, k in zip(state, intervals)]
        for m in range(M):
            state = [stencil(cf, 0, u) for u in state]
        for u, k in zip(state, intervals):
            rd[k] = u
        return relaxed, state

    err, entry = None, None
    for intervals in ((0, 1, 2, 3, 4, 5, 6, 7),):
        relaxed, resid = fine(intervals)
        if err is None:
            entry = jnp.where(z == 0, relaxed[0] - relaxed[0], zero)
            err = entry
        for k in range(0, len(intervals), 2):
            err = coarse_two(cf, err, resid[k], resid[k + 1])[1]
    lw[0] = err

    def send_main(packed, plane, slot, sem):
        pltpu.make_async_remote_copy(
            packed, lr.at[slot, pl.ds(1, 2)], s2.at[sem], r2.at[slot], at(plane, here), pl.DeviceIdType.MESH
        ).start()

    def send_sides(packed, plane, slot, sem):
        for src, part, side in ((packed.at[0], 3, lo), (packed.at[1], 0, hi)):
            pltpu.make_async_remote_copy(
                src, lr.at[slot, part], s2.at[sem], r2.at[slot], at(plane, side), pl.DeviceIdType.MESH
            ).start()

    def send_three(packed, plane, slot, sem):
        send_main(packed, plane, slot, sem)
        send_sides(packed, plane, slot, sem)

    def send_window(window, plane, slot, sem):
        pltpu.make_async_remote_copy(
            window, ul.at[slot], s2.at[sem], r4.at[slot], at(plane, here), pl.DeviceIdType.MESH
        ).start()

    def window_arrived(slot):
        pltpu.make_async_copy(ul.at[slot], ul.at[slot], r4.at[slot]).wait()

    def arrived(slot):
        pltpu.make_async_copy(lr.at[slot], lr.at[slot], r2.at[slot]).wait()
        return unpack_window([lr[slot, h] for h in range(4)])

    lane64 = lane_ids(64)

    def send_results(xx):
        for offset in OFFSETS:
            if offset[0] == 0 and offset != OFFSETS[-1]:
                ps = mates[offset][1]
                pltpu.make_async_remote_copy(
                    po.at[xx, pl.ds(8 * ps, 8)], ob.at[c], s3, r3, (z * NX_DEV + xx, ps), pl.DeviceIdType.MESH
                ).start()
        mine_out = po.at[xx, pl.ds(8 * s, 8)]

        @pl.when(x == xx)
        def _():
            pltpu.make_async_copy(mine_out, ob.at[c], r3).start()

        @pl.when(x != xx)
        def _():
            pltpu.make_async_remote_copy(
                mine_out, ob.at[c], s3, r3, (z * NX_DEV + xx, s), pl.DeviceIdType.MESH
            ).start()

    def chain(err, ready_made):
        for xx in range(NX_DEV):
            first = rx[2 * xx] + err
            mid, err = coarse_two(cf, err, rd[2 * xx], rd[2 * xx + 1])
            second = rx[2 * xx + 1] + mid
            po[xx] = jnp.where(lane64 < 64, pltpu.roll(first, 96, 1), pltpu.roll(second, 32, 1))
            ready_made(xx)
        return err

    @pl.when(z == 0)
    def _():
        def pass_on(e, which, planes):
            pack_halves(e, pe.at[which])
            for plane in planes:
                send_three(pe.at[which], plane, 0, plane)

        pack_halves(lw[0], pk)
        send_sides(pk, 0, 0, 0)
        pltpu.make_async_copy(pk, lr.at[0, pl.ds(1, 2)], r2.at[0]).start()
        pl.semaphore_wait(ready.at[1], 1)
        send_window(lw.at[0], 1, 0, 1)
        chain(entry, send_results)
        square_coarse(cf, kf)
        for plane in range(2, NZ):
            pl.semaphore_wait(ready.at[plane], 1 if plane < 4 else 3)
        e = arrived(0)
        for j in range(1, 3):
            e = coarse_eight(kf, e)
            window_arrived(j - 1)
            e = e + ul[j - 1]
            lw[j] = e
            send_window(lw.at[j], j + 1, 0, j + 1)
        pass_on(e, 0, (5, 4, 6))
        pass_on(coarse_eight(kf, e), 1, (7,))

    @pl.when(jnp.logical_and(z >= 1, z <= 2))
    def _():
        send_window(lw.at[0], 0, z - 1, 1)

    @pl.when(jnp.logical_or(z == 3, z == 4))
    def _():
        pack_halves(lw[0], pk)

    @pl.when(z == 3)
    def _():
        for plane in range(4, NZ):
            pl.semaphore_wait(ready.at[plane], 1 if plane < 6 else 3)
        send_three(pk, 7, 2, 7)

    for plane in (7, 6, 5, 4):
        if plane >= 6:

            @pl.when(z == plane - 3)
            def _(plane=plane):
                send_three(pk, plane, 1, plane)

        @pl.when(jnp.logical_and(z >= (3 if plane < 6 else plane - 2), z < plane))
        def _(plane=plane):
            send_window(lw.at[0], plane, z - (4 if plane == 7 else 3), plane)

    @pl.when(z >= 4)
    def _():
        square_coarse(cf, kf)

    for slot in range(3):

        @pl.when((z == 4) | (z == 5) if slot == 0 else z >= 4 + slot)
        def _(slot=slot):
            window_arrived(slot)

    @pl.when(z >= 6)
    def _():
        ul[0] = arrived(1)

    ahead_3[...] = zero

    @pl.when(z == 7)
    def _():
        ahead_3[...] = arrived(2)

    @pl.when(jnp.logical_and(z >= 1, z <= 3))
    def _():
        window_arrived(0)
        e_in[...] = ul[0]

    @pl.when(z >= 4)
    def _():
        e_in[...] = lax.fori_loop(
            0, jnp.minimum(z - 3, 3), lambda j, e: coarse_eight(kf, e) + ul[j], arrived(0) + ahead_3[...]
        )

    @pl.when(z > 0)
    def _():
        chain(e_in[...], send_results)

    pltpu.make_async_copy(ob, ob, r3).wait()

    sent = sb.at[pl.ds(0, STRIPS - 1)]
    pltpu.make_async_copy(sent, sent, s1).wait()
    sent_fields = sf.at[pl.ds(0, NS - 1)]
    pltpu.make_async_copy(sent_fields, sent_fields, s0).wait()

    @pl.when(gives_next)
    def _():
        pltpu.make_async_copy(sp, sp, sq).wait()

    @pl.when(gives_first)
    def _():
        most = sp.at[pl.ds(0, STRIPS - 1)]
        pltpu.make_async_copy(most, most, sq).wait()

    @pl.when(z == 0)
    def _():
        pltpu.make_async_copy(pk, pk, s2.at[0]).wait()
        for plane in range(1, NZ):
            pltpu.make_async_copy(lr.at[0], lr.at[0], s2.at[plane]).wait()

    @pl.when(jnp.logical_and(z >= 1, z <= 2))
    def _():
        pltpu.make_async_copy(lr.at[0], lr.at[0], s2.at[1]).wait()

    for plane in (7, 6, 5, 4):

        @pl.when(jnp.logical_and(z >= 3, z < plane))
        def _(plane=plane):
            pltpu.make_async_copy(lr.at[0], lr.at[0], s2.at[plane]).wait()

    gone = ob.at[pl.ds(0, STRIPS - 1)]
    pltpu.make_async_copy(gone, gone, s3).wait()


def place_rows(ob, out):
    lane8 = lane_ids(8)
    for p in range(16):
        left, right = ob[2 * p], ob[2 * p + 1]
        here = slice(LANES * p, LANES * (p + 1))
        out[0, :, here] = jnp.where(lane8 < 64, left, pltpu.roll(right, 64, 1))
        out[1, :, here] = jnp.where(lane8 < 64, pltpu.roll(left, 64, 1), right)


def per_device(*blocks):
    any_space = pl.BlockSpec(memory_space=pl.ANY)
    f32 = functools.partial(pltpu.VMEM, dtype=jnp.float32)
    sem = pltpu.SemaphoreType.DMA
    strips = pl.pallas_call(
        kernel,
        out_shape=jax.ShapeDtypeStruct((STRIPS, 8, LANES), jnp.float32),
        in_specs=[any_space] * 7,
        out_specs=any_space,
        scratch_shapes=[
            pltpu.SMEM((8,), jnp.float32),
            f32((2, 8, 2048)),
            f32((4, 8, 2048)),
            f32((8, 2048)),
            f32((STRIPS, 2, 8, LANES)),
            f32((NS, 4, 8, LANES)),
            f32((STRIPS, 8, LANES)),
            f32((8, 64, LANES)),
            f32((4, 64, LANES)),
            f32((64, LANES)),
            f32((20, 64, LANES)),
            f32((13, 64, LANES)),
            f32((8, 64, LANES)),
            f32((8, 64, LANES)),
            f32((2, 16, LANES)),
            f32((2, 2, 16, LANES)),
            f32((3, 4, 16, LANES)),
            f32((3, 64, LANES)),
            f32((3, 64, LANES)),
            f32((64, LANES)),
            f32((64, LANES)),
            f32((NX_DEV, 64, LANES)),
            sem((8,)),
            sem,
            sem,
            sem,
            sem,
            sem,
            sem,
            sem((8,)),
            sem((3,)),
            sem((3,)),
            sem,
            sem,
            pltpu.SemaphoreType.REGULAR((NZ,)),
        ],
        compiler_params=pltpu.CompilerParams(
            collective_id=0, has_side_effects=True, vmem_limit_bytes=56 * 1024 * 1024
        ),
        cost_estimate=pl.CostEstimate(flops=20_000_000, bytes_accessed=700_000, transcendentals=0),
        name="cycle",
    )(*blocks)
    in_vmem = pl.BlockSpec(memory_space=pltpu.VMEM)
    return pl.pallas_call(
        place_rows,
        out_shape=jax.ShapeDtypeStruct((2, 8, 2048), jnp.float32),
        in_specs=[in_vmem],
        out_specs=in_vmem,
        name="place",
    )(strips)


def solution(mesh):
    in_specs = (
        P("space", None),
        P("space", None),
        P("space", None),
        P("space", None),
        P("space", None),
        P("tm"),
        P("tm", "space", None),
    )
    out_specs = P("tm", "space", None)
    return jax.shard_map(
        per_device, mesh=mesh, in_specs=in_specs, out_specs=out_specs, check_vma=False
    )
```

```python
import functools

import jax
import jax.numpy as jnp
from jax import lax
from jax.experimental import pallas as pl
from jax.experimental.pallas import tpu as pltpu
from jax.sharding import PartitionSpec as P

M = 4
NZ = 8
NX_DEV = 4
NS = 8
STRIPS = 32
LANES = 128


OFFSETS = sorted(
    ((dx, dy, dc) for dx in range(4) for dy in range(4) for dc in range(2)),
    key=lambda o: (-min(o[0], 4 - o[0]) - min(o[1], 4 - o[1]), -o[2]),
)


def div(a, b):
    return lax.div(a, jnp.int32(b))


def rem(a, b):
    return lax.rem(a, jnp.int32(b))


def place_of(strip):
    chip, core = div(strip, 2), rem(strip, 2)
    y, q = div(chip, 4), rem(chip, 4)
    x = q + rem(y, 2) * (3 - 2 * q)
    return x, 2 * y + core


def strip_of(x, s):
    y, core = div(s, 2), rem(s, 2)
    q = x + rem(y, 2) * (3 - 2 * x)
    return 2 * (4 * y + q) + core


def lane_ids(rows):
    return lax.broadcasted_iota(jnp.int32, (rows, LANES), 1)


def pack_halves(value, out_ref):
    lane = lane_ids(16)
    for half in range(2):
        block = 1 + half
        packed = None
        for group in range(4):
            piece = value[16 * group : 16 * group + 16]
            shift = (32 * (group - block)) % LANES
            moved = piece if shift == 0 else pltpu.roll(piece, shift, 1)
            packed = moved if packed is None else jnp.where(lane < 32 * group, packed, moved)
        out_ref[half] = packed


def unpack_window(parts):
    lane = lane_ids(16)
    rows = []
    for group in range(4):
        row = None
        for block in range(4):
            shift = (32 * (block - group)) % LANES
            moved = parts[block] if shift == 0 else pltpu.roll(parts[block], shift, 1)
            row = moved if row is None else jnp.where(lane < 32 * block, row, moved)
        rows.append(row)
    return jnp.concatenate(rows, axis=0)


def point(cf, base, mid, left, right):
    near = cf[base] * mid + cf[base + 1] * pltpu.roll(mid, 1, 0) + cf[base + 2] * pltpu.roll(mid, 63, 0)
    return near + (cf[base + 3] * left + cf[base + 4] * right)


def lanes(u, steps):
    return pltpu.roll(u, steps % LANES, 1)


def stencil(cf, base, u):
    return point(cf, base, u, lanes(u, 1), lanes(u, -1))


def coarse_two(cf, u, r1=None, r2=None):
    left, left2, right, right2 = lanes(u, 1), lanes(u, 2), lanes(u, -1), lanes(u, -2)
    v = point(cf, 5, u, left, right)
    v_left = point(cf, 10, left, left2, u)
    v_right = point(cf, 15, right, u, right2)
    if r1 is not None:
        v, v_left, v_right = v + r1, v_left + lanes(r1, 1), v_right + lanes(r1, -1)
    w = point(cf, 5, v, v_left, v_right)
    if r2 is not None:
        w = w + r2
    return v, w


def square_coarse(cf, kf):
    mid, up, down, left, right = (cf[5 + k] for k in range(5))
    at_left, at_right = [cf[10 + k] for k in range(5)], [cf[15 + k] for k in range(5)]
    at_up = [pltpu.roll(cf[5 + k], 1, 0) for k in range(5)]
    at_down = [pltpu.roll(cf[5 + k], 63, 0) for k in range(5)]
    kf[0] = (mid * mid + up * at_up[2] + down * at_down[1]) + (left * at_left[4] + right * at_right[3])
    kf[1] = left * (mid + at_left[0])
    kf[2] = right * (mid + at_right[0])
    kf[3] = left * at_left[3]
    kf[4] = right * at_right[4]
    kf[5] = pltpu.roll(up * at_up[1], 62, 0)
    kf[6] = pltpu.roll(down * at_down[2], 2, 0)
    kf[7] = pltpu.roll(up * (mid + at_up[0]), 63, 0)
    kf[8] = pltpu.roll(up * at_up[3] + left * at_left[1], 63, 0)
    kf[9] = pltpu.roll(up * at_up[4] + right * at_right[1], 63, 0)
    kf[10] = pltpu.roll(down * (mid + at_down[0]), 1, 0)
    kf[11] = pltpu.roll(down * at_down[3] + left * at_left[2], 1, 0)
    kf[12] = pltpu.roll(down * at_down[4] + right * at_right[2], 1, 0)


def coarse_square(kf, u):
    left, left2, right, right2 = lanes(u, 1), lanes(u, 2), lanes(u, -1), lanes(u, -2)
    above = kf[7] * u + (kf[8] * left + kf[9] * right)
    below = kf[10] * u + (kf[11] * left + kf[12] * right)
    far = pltpu.roll(kf[5] * u, 2, 0) + pltpu.roll(kf[6] * u, 62, 0)
    row = (kf[1] * left + kf[2] * right) + (kf[3] * left2 + kf[4] * right2)
    return (kf[0] * u + far + row) + (pltpu.roll(above, 1, 0) + pltpu.roll(below, 63, 0))


def coarse_eight(kf, u):
    for _ in range(4):
        u = coarse_square(kf, u)
    return u


def kernel(
    initial, source, rate, velx, vely, strengths, guess, ob,
    amp, gb, fb, ib, sb, sf, sp, rb, rp, pb, cf, kf, rx, rd, pk, pe, lr, ul, lw, e_in, ahead_3, po,
    ld, s1, r1, s0, r0, sq, rq, s2, r2, r4, s3, r3, ready,
):
    t, s = lax.axis_index("tm"), lax.axis_index("space")
    z, x = div(t, NX_DEV), rem(t, NX_DEV)
    c = strip_of(x, s)
    lo, here, hi = place_of(rem(c + STRIPS - 1, STRIPS)), (x, s), place_of(rem(c + 1, STRIPS))
    xs = [rem(x + dx, NX_DEV) for dx in range(NX_DEV)]
    other = 1 - 2 * rem(s, 2)
    ss = [rem(s + 2 * dy, NS) for dy in range(4)]
    mates = {(dx, dy, dc): (xs[dx], ss[dy] + other * dc) for dx, dy, dc in OFFSETS}

    gives_next = jnp.logical_and(x == NX_DEV - 1, z < NZ - 1)
    gives_first = jnp.logical_and(x == 0, z == 0)
    gives = jnp.logical_or(gives_next, gives_first)

    def at(plane, place):
        return (plane * NX_DEV + place[0], place[1])

    barrier = pltpu.get_barrier_semaphore()

    def greet(device):
        pl.semaphore_signal(barrier, inc=1, device_id=device, device_id_type=pl.DeviceIdType.MESH)

    for offset in OFFSETS[:-1]:
        px, ps = mates[offset]
        greet((z * NX_DEV + px, ps))

    def greet_before(i, _):
        greet(((z - 1) * NX_DEV + NX_DEV - 1, i))
        return 0

    lax.fori_loop(0, jnp.where(z > 0, NS, 0), greet_before, 0)

    def greet_three(plane):
        greet(at(plane, lo))
        greet(at(plane, here))
        greet(at(plane, hi))

    @pl.when(z == 0)
    def _():
        for plane in range(1, 4):
            greet(at(plane, here))
        for plane in range(4, NZ):
            greet_three(plane)

    def greet_upper(plane, _):
        greet(at(plane, here))
        return 0

    lax.fori_loop(4, jnp.maximum(z, 4), greet_upper, 0)

    @pl.when(z == 7)
    def _():
        greet(at(4, lo))
        greet(at(4, hi))

    @pl.when(z == 3)
    def _():
        greet(at(4, here))
        greet(at(5, here))
        greet_three(6)
        greet_three(7)

    load_guess = pltpu.make_async_copy(guess, gb, ld.at[0])
    load_guess.start()
    load_amp = pltpu.make_async_copy(strengths, amp, ld.at[3])
    load_amp.start()
    load_fields = [
        pltpu.make_async_copy(field, fb.at[which], ld.at[4 + which])
        for which, field in enumerate((rate, velx, vely, source))
    ]
    for load in load_fields:
        load.start()

    @pl.when(gives_first)
    def _():
        pltpu.make_async_copy(initial, ib, ld.at[2]).start()

    @pl.when(gives_next)
    def _():
        pltpu.make_async_copy(guess.at[1], ib, ld.at[2]).start()

    load_guess.wait()
    load_amp.wait()

    lane8 = lane_ids(8)

    def windows(tile_of, put):
        low = [pltpu.roll(tile_of(k), 32, 1) for k in range(16)]
        for k in range(16):
            put(2 * k, jnp.where(lane8 < 32, low[k - 1], low[k]))
        high = [pltpu.roll(tile_of(k), 96, 1) for k in range(16)]
        for k in range(16):
            put(2 * k + 1, jnp.where(lane8 < 96, high[k], high[(k + 1) % 16]))

    for i in range(2):

        def put_guess(strip, value, i=i):
            for m in range(M):
                value = jnp.where(lane8 == m, amp[M * i + m], value)
            sb[strip, i] = value

        windows(lambda k, i=i: gb[i, :, LANES * k : LANES * (k + 1)], put_guess)

    for load in load_fields:
        load.wait()
    for y in range(4):
        k = 4 * y + (x if y % 2 == 0 else 3 - x)
        k_lo, k_at, k_hi = (
            pl.ds(pl.multiple_of(LANES * ((k + move) % 16), LANES), LANES) for move in (15, 0, 1)
        )
        for f in range(4):
            tile = fb[f, :, k_at]
            sf[2 * y, f] = jnp.where(
                lane8 < 32, pltpu.roll(fb[f, :, k_lo], 32, 1), pltpu.roll(tile, 32, 1)
            )
            sf[2 * y + 1, f] = jnp.where(
                lane8 < 96, pltpu.roll(tile, 96, 1), pltpu.roll(fb[f, :, k_hi], 96, 1)
            )

    @pl.when(gives)
    def _():
        pltpu.make_async_copy(initial, ib, ld.at[2]).wait()

        def put_before(strip, value):
            sp[strip] = value

        windows(lambda k: ib[:, LANES * k : LANES * (k + 1)], put_before)

    hubs = jnp.where(z == 0, 0, jnp.where(z < 4, 1, 3))
    uppers = jnp.where(z == 4, 5, jnp.where(z == 5, 2, jnp.where(z == 6, 1, 0)))
    from_3 = jnp.where(z >= 6, 3, jnp.where(z >= 4, 1, 0))
    pl.semaphore_wait(barrier, STRIPS - 1 + jnp.where(gives_next, STRIPS, 0) + hubs + uppers + from_3)

    def signal_ready(place, plane=0):
        pl.semaphore_signal(
            ready.at[z], inc=1, device_id=at(plane, place), device_id_type=pl.DeviceIdType.MESH
        )

    @pl.when(z > 0)
    def _():
        signal_ready(here)

    @pl.when(z >= 4)
    def _():
        signal_ready(lo)
        signal_ready(hi)
        signal_ready(here, 3)

    @pl.when(z >= 6)
    def _():
        signal_ready(lo, 3)
        signal_ready(hi, 3)

    mine = rb.at[pl.ds(2 * x, 2), pl.ds(8 * s, 8)]
    mine_fields = rp.at[:, pl.ds(8 * s, 8)]

    ahead = pb.at[pl.ds(8 * s, 8)]

    @pl.when(gives)
    def _():
        to = jnp.where(gives_next, z + 1, 0)

        def give(offset):
            px, ps = mates[offset]
            pltpu.make_async_remote_copy(
                sp.at[strip_of(px, ps)], ahead, sq, rq, (to * NX_DEV + px, ps), pl.DeviceIdType.MESH
            ).start()

        for offset in OFFSETS[:-1]:
            give(offset)

        @pl.when(gives_next)
        def _():
            give(OFFSETS[-1])

        @pl.when(gives_first)
        def _():
            pltpu.make_async_copy(sp.at[c], ahead, rq).start()

    for offset in OFFSETS[:-1]:
        px, ps = mates[offset]
        if offset[0] == 0:
            pltpu.make_async_remote_copy(
                sf.at[ps], mine_fields, s0, r0, (z * NX_DEV + px, ps), pl.DeviceIdType.MESH
            ).start()
    for offset in OFFSETS[:-1]:
        px, ps = mates[offset]
        pltpu.make_async_remote_copy(
            sb.at[strip_of(px, ps)], mine, s1, r1, (z * NX_DEV + px, ps), pl.DeviceIdType.MESH
        ).start()
    pltpu.make_async_copy(sb.at[c], mine, r1).start()
    pltpu.make_async_copy(sf.at[s], mine_fields, r0).start()
    pltpu.make_async_copy(rp, rp, r0).wait()

    d, a, b = rp[0], rp[1], rp[2]
    row = lax.broadcasted_iota(jnp.int32, (64, LANES), 0)
    col = lax.broadcasted_iota(jnp.int32, (64, LANES), 1) + (64 * c - 32)
    zero = jnp.zeros((64, LANES), jnp.float32)
    c_mid = 1.0 - (4.0 * d + (jnp.abs(a) + jnp.abs(b)))
    c_xm = jnp.where(row == 0, zero, d + jnp.maximum(a, 0.0))
    c_xp = jnp.where(row == 63, zero, d - jnp.minimum(a, 0.0))
    c_ym = jnp.where(col == 0, zero, d + jnp.maximum(b, 0.0))
    c_yp = jnp.where(col == 2047, zero, d - jnp.minimum(b, 0.0))
    cf[0], cf[1], cf[2], cf[3], cf[4] = c_mid, c_xm, c_xp, c_ym, c_yp
    cf[5] = 1.0 - float(M) * (4.0 * d + (jnp.abs(a) + jnp.abs(b)))
    cf[6], cf[7], cf[8], cf[9] = M * c_xm, M * c_xp, M * c_ym, M * c_yp
    for k in range(5):
        cf[10 + k] = lanes(cf[5 + k], 1)
        cf[15 + k] = lanes(cf[5 + k], -1)

    pltpu.make_async_copy(rb, rb, r1).wait()
    pltpu.make_async_copy(pb, pb, rq).wait()

    def forced(u, tile, m):
        strength = jnp.broadcast_to(rb[tile, 0:8, m : m + 1], (8, LANES))
        push = rp[3].reshape(8, 8, LANES) * strength[None]
        return stencil(cf, 0, u) + push.reshape(64, LANES)

    def fine(intervals):
        state = [pb[...] if k == 0 else rb[k - 1] for k in intervals]
        for m in range(M):
            state = [forced(u, k, m) for u, k in zip(state, intervals)]
        relaxed = state
        for u, k in zip(relaxed, intervals):
            rx[k] = u
        state = [u - rb[k] for u, k in zip(state, intervals)]
        for m in range(M):
            state = [stencil(cf, 0, u) for u in state]
        for u, k in zip(state, intervals):
            rd[k] = u
        return relaxed, state

    err, entry = None, None
    for intervals in ((0, 1, 2, 3, 4, 5, 6, 7),):
        relaxed, resid = fine(intervals)
        if err is None:
            entry = jnp.where(z == 0, relaxed[0] - relaxed[0], zero)
            err = entry
        for k in range(0, len(intervals), 2):
            err = coarse_two(cf, err, resid[k], resid[k + 1])[1]
    lw[0] = err

    def send_main(packed, plane, slot, sem):
        pltpu.make_async_remote_copy(
            packed, lr.at[slot, pl.ds(1, 2)], s2.at[sem], r2.at[slot], at(plane, here), pl.DeviceIdType.MESH
        ).start()

    def send_sides(packed, plane, slot, sem):
        for src, part, side in ((packed.at[0], 3, lo), (packed.at[1], 0, hi)):
            pltpu.make_async_remote_copy(
                src, lr.at[slot, part], s2.at[sem], r2.at[slot], at(plane, side), pl.DeviceIdType.MESH
            ).start()

    def send_three(packed, plane, slot, sem):
        send_main(packed, plane, slot, sem)
        send_sides(packed, plane, slot, sem)

    def send_window(window, plane, slot, sem):
        pltpu.make_async_remote_copy(
            window, ul.at[slot], s2.at[sem], r4.at[slot], at(plane, here), pl.DeviceIdType.MESH
        ).start()

    def window_arrived(slot):
        pltpu.make_async_copy(ul.at[slot], ul.at[slot], r4.at[slot]).wait()

    def arrived(slot):
        pltpu.make_async_copy(lr.at[slot], lr.at[slot], r2.at[slot]).wait()
        return unpack_window([lr[slot, h] for h in range(4)])

    lane64 = lane_ids(64)

    def send_results(xx):
        for offset in OFFSETS:
            if offset[0] == 0 and offset != OFFSETS[-1]:
                ps = mates[offset][1]
                pltpu.make_async_remote_copy(
                    po.at[xx, pl.ds(8 * ps, 8)], ob.at[c], s3, r3, (z * NX_DEV + xx, ps), pl.DeviceIdType.MESH
                ).start()
        mine_out = po.at[xx, pl.ds(8 * s, 8)]

        @pl.when(x == xx)
        def _():
            pltpu.make_async_copy(mine_out, ob.at[c], r3).start()

        @pl.when(x != xx)
        def _():
            pltpu.make_async_remote_copy(
                mine_out, ob.at[c], s3, r3, (z * NX_DEV + xx, s), pl.DeviceIdType.MESH
            ).start()

    def chain(err, ready_made):
        for xx in range(NX_DEV):
            first = rx[2 * xx] + err
            mid, err = coarse_two(cf, err, rd[2 * xx], rd[2 * xx + 1])
            second = rx[2 * xx + 1] + mid
            po[xx] = jnp.where(lane64 < 64, pltpu.roll(first, 96, 1), pltpu.roll(second, 32, 1))
            ready_made(xx)
        return err

    @pl.when(z == 0)
    def _():
        def pass_on(e, which, planes):
            pack_halves(e, pe.at[which])
            for plane in planes:
                send_three(pe.at[which], plane, 0, plane)

        pack_halves(lw[0], pk)
        send_sides(pk, 0, 0, 0)
        pltpu.make_async_copy(pk, lr.at[0, pl.ds(1, 2)], r2.at[0]).start()
        pl.semaphore_wait(ready.at[1], 1)
        send_window(lw.at[0], 1, 0, 1)
        chain(entry, send_results)
        square_coarse(cf, kf)
        for plane in range(2, NZ):
            pl.semaphore_wait(ready.at[plane], 1 if plane < 4 else 3)
        e = arrived(0)
        for j in range(1, 3):
            e = coarse_eight(kf, e)
            window_arrived(j - 1)
            e = e + ul[j - 1]
            lw[j] = e
            send_window(lw.at[j], j + 1, 0, j + 1)
        pass_on(e, 0, (5, 4, 6))
        pass_on(coarse_eight(kf, e), 1, (7,))

    @pl.when(jnp.logical_and(z >= 1, z <= 2))
    def _():
        send_window(lw.at[0], 0, z - 1, 1)

    @pl.when(jnp.logical_or(z == 3, z == 4))
    def _():
        pack_halves(lw[0], pk)

    @pl.when(z == 3)
    def _():
        for plane in range(4, NZ):
            pl.semaphore_wait(ready.at[plane], 1 if plane < 6 else 3)
        send_three(pk, 7, 2, 7)

    for plane in (7, 6, 5, 4):
        if plane >= 6:

            @pl.when(z == plane - 3)
            def _(plane=plane):
                send_three(pk, plane, 1, plane)

        @pl.when(jnp.logical_and(z >= (3 if plane < 6 else plane - 2), z < plane))
        def _(plane=plane):
            send_window(lw.at[0], plane, z - (4 if plane == 7 else 3), plane)

    @pl.when(z >= 4)
    def _():
        square_coarse(cf, kf)

    for slot in range(3):

        @pl.when((z == 4) | (z == 5) if slot == 0 else z >= 4 + slot)
        def _(slot=slot):
            window_arrived(slot)

    @pl.when(z >= 6)
    def _():
        ul[0] = arrived(1)

    ahead_3[...] = zero

    @pl.when(z == 7)
    def _():
        ahead_3[...] = arrived(2)

    @pl.when(jnp.logical_and(z >= 1, z <= 3))
    def _():
        window_arrived(0)
        e_in[...] = ul[0]

    @pl.when(z >= 4)
    def _():
        e_in[...] = lax.fori_loop(
            0, jnp.minimum(z - 3, 3), lambda j, e: coarse_eight(kf, e) + ul[j], arrived(0) + ahead_3[...]
        )

    @pl.when(z > 0)
    def _():
        chain(e_in[...], send_results)

    sent = sb.at[pl.ds(0, STRIPS - 1)]
    pltpu.make_async_copy(sent, sent, s1).wait()
    sent_fields = sf.at[pl.ds(0, NS - 1)]
    pltpu.make_async_copy(sent_fields, sent_fields, s0).wait()

    @pl.when(gives_next)
    def _():
        pltpu.make_async_copy(sp, sp, sq).wait()

    @pl.when(gives_first)
    def _():
        most = sp.at[pl.ds(0, STRIPS - 1)]
        pltpu.make_async_copy(most, most, sq).wait()

    @pl.when(z == 0)
    def _():
        pltpu.make_async_copy(pk, pk, s2.at[0]).wait()
        for plane in range(1, NZ):
            pltpu.make_async_copy(lr.at[0], lr.at[0], s2.at[plane]).wait()

    @pl.when(jnp.logical_and(z >= 1, z <= 2))
    def _():
        pltpu.make_async_copy(lr.at[0], lr.at[0], s2.at[1]).wait()

    for plane in (7, 6, 5, 4):

        @pl.when(jnp.logical_and(z >= 3, z < plane))
        def _(plane=plane):
            pltpu.make_async_copy(lr.at[0], lr.at[0], s2.at[plane]).wait()

    gone = ob.at[pl.ds(0, STRIPS - 1)]
    pltpu.make_async_copy(gone, gone, s3).wait()
    pltpu.make_async_copy(ob, ob, r3).wait()


def place_rows(ob, out):
    lane8 = lane_ids(8)
    for p in range(16):
        left, right = ob[2 * p], ob[2 * p + 1]
        here = slice(LANES * p, LANES * (p + 1))
        out[0, :, here] = jnp.where(lane8 < 64, left, pltpu.roll(right, 64, 1))
        out[1, :, here] = jnp.where(lane8 < 64, pltpu.roll(left, 64, 1), right)


def per_device(*blocks):
    any_space = pl.BlockSpec(memory_space=pl.ANY)
    f32 = functools.partial(pltpu.VMEM, dtype=jnp.float32)
    sem = pltpu.SemaphoreType.DMA
    strips = pl.pallas_call(
        kernel,
        out_shape=jax.ShapeDtypeStruct((STRIPS, 8, LANES), jnp.float32),
        in_specs=[any_space] * 7,
        out_specs=any_space,
        scratch_shapes=[
            pltpu.SMEM((8,), jnp.float32),
            f32((2, 8, 2048)),
            f32((4, 8, 2048)),
            f32((8, 2048)),
            f32((STRIPS, 2, 8, LANES)),
            f32((NS, 4, 8, LANES)),
            f32((STRIPS, 8, LANES)),
            f32((8, 64, LANES)),
            f32((4, 64, LANES)),
            f32((64, LANES)),
            f32((20, 64, LANES)),
            f32((13, 64, LANES)),
            f32((8, 64, LANES)),
            f32((8, 64, LANES)),
            f32((2, 16, LANES)),
            f32((2, 2, 16, LANES)),
            f32((3, 4, 16, LANES)),
            f32((3, 64, LANES)),
            f32((3, 64, LANES)),
            f32((64, LANES)),
            f32((64, LANES)),
            f32((NX_DEV, 64, LANES)),
            sem((8,)),
            sem,
            sem,
            sem,
            sem,
            sem,
            sem,
            sem((8,)),
            sem((3,)),
            sem((3,)),
            sem,
            sem,
            pltpu.SemaphoreType.REGULAR((NZ,)),
        ],
        compiler_params=pltpu.CompilerParams(
            collective_id=0, has_side_effects=True, vmem_limit_bytes=56 * 1024 * 1024
        ),
        cost_estimate=pl.CostEstimate(flops=20_000_000, bytes_accessed=700_000, transcendentals=0),
        name="cycle",
    )(*blocks)
    in_vmem = pl.BlockSpec(memory_space=pltpu.VMEM)
    return pl.pallas_call(
        place_rows,
        out_shape=jax.ShapeDtypeStruct((2, 8, 2048), jnp.float32),
        in_specs=[in_vmem],
        out_specs=in_vmem,
        name="place",
    )(strips)


def solution(mesh):
    in_specs = (
        P("space", None),
        P("space", None),
        P("space", None),
        P("space", None),
        P("space", None),
        P("tm"),
        P("tm", "space", None),
    )
    out_specs = P("tm", "space", None)
    return jax.shard_map(
        per_device, mesh=mesh, in_specs=in_specs, out_specs=out_specs, check_vma=False
    )
```
